32 devices in a mesh: file: 16 (over z, y, core), win: 2 (over x).
Axes of the slice: x: 2, y: 2, z: 4, core: 2. Of those that a mesh axis runs over, the one named last changes fastest.
Arguments:
- raw: bfloat16 [2, 128, 20480], P('win', None, 'file'), may hold values from -60 to 60
- fir_taps: float32 [64], replicated, may hold values from -0.75 to 0.75
- offsets: int32 [2, 16], P('win', 'file'), may hold values from 0 to 9
- vs_index: int32 [64], replicated, may hold values from 0 to 127, as said below
Outputs:
- correlation: float32 [64, 128, 2048], P('win', 'file')
The draws below stay inside these ranges and needn't reach their ends.
Inputs may be any that keep to these rules, and one draw needn't show every extreme that they name: `vs_index`: virtual source s is one of the channels s * 2 to s * 2 + 1.
All inputs are finite; a program needn't handle non-finite values.
Results may differ from the reference program's by a relative error of at most 0.0063.
Values may be sent and summed in bfloat16 or wider, within the bound.
No kernel may reach another device: no remote copies, remote signals or barrier semaphores. Data moves between devices by JAX's collectives and lax.ppermute only.
A program may use at most 128 MiB of HBM per device.

```python
import math
import jax
import jax.numpy as jnp
from jax import lax

R = 10
TAPS = 64
TD = 128
SEG = 2048
BAND = 64
STRIDE = 2
NFILE = 16
NWIN = 2
CH = 128
NVS = 64
TR = 1280
SAMP = 20480
NT = 2048
NSEG = 1


def draw_raw(key, part):
    noise_key = jax.random.fold_in(key, 11)
    scale_key = jax.random.fold_in(key, 12)
    levels = jnp.exp(jax.random.uniform(scale_key, (NWIN, CH, 1), jnp.float32, 0.0, math.log(10.0)))
    noise = jnp.clip(jax.random.normal(noise_key, (NWIN, CH, SAMP), jnp.float32), -6.0, 6.0)
    return (noise * levels).astype(jnp.bfloat16)


def draw_vs_index(key, part):
    jitter = jax.random.randint(jax.random.fold_in(key, 21), (NVS,), 0, STRIDE).astype(jnp.int32)
    jitter = jitter.at[0].set(0).at[NVS - 1].set(STRIDE - 1)
    return jnp.arange(NVS, dtype=jnp.int32) * STRIDE + jitter


def touch_ends(entries, key, smallest, high):
    shape = entries.shape
    place = [jax.random.randint(jax.random.fold_in(key, axis), (), 0, shape[axis]) for axis in range(len(shape))]
    entries = entries.at[tuple(place)].set(smallest)
    longest = shape.index(max(shape))
    place[longest] = (place[longest] + 1) % shape[longest]
    return entries.at[tuple(place)].set(high)


def scatter_about(rng, extent, width, limit, kind=jnp.bfloat16):
    values = width * jax.random.normal(rng, extent, jnp.float32)
    return jnp.clip(values, min=-limit, max=limit).astype(kind)


def setup_inputs(seed: int = 0) -> dict:
    key_list = jax.random.split(jax.random.key(seed), 5)
    return {
        "raw": draw_raw(jax.random.fold_in(key_list[4], 71), 0),
        "fir_taps": scatter_about(key_list[1], (TAPS,), TAPS ** -0.5, 0.75, jnp.float32),
        "offsets": touch_ends(jax.random.randint(key_list[2], (NWIN, NFILE), 0, R), jax.random.fold_in(key_list[2], 1), 0, R - 1).astype(jnp.int32),
        "vs_index": draw_vs_index(jax.random.fold_in(key_list[4], 71), 0),
    }


EPSILON = 1e-06

def decimate_window(raw_window, taps_wide, file_shifts):
    file_blocks = raw_window.reshape(CH, NT // TD, TR)
    previous = jnp.concatenate([jnp.zeros((CH, 1, TAPS), raw_window.dtype), file_blocks[:, :-1, TR - TAPS:]], axis=1)
    extended = jnp.concatenate([previous, file_blocks], axis=2)
    outputs = jnp.arange(TD, dtype=jnp.int32)
    lagged = jnp.arange(TAPS, dtype=jnp.int32)

    def one_file(operands):
        file_block, offset_now = operands
        picks = (TAPS + offset_now + R * outputs[:, None] - lagged[None, :]).astype(jnp.int32)
        gathered = file_block[:, picks].astype(jnp.float32)
        return jnp.einsum('cjk,k->cj', gathered, taps_wide)
    result = lax.map(one_file, (jnp.moveaxis(extended, 1, 0), file_shifts))
    return jnp.moveaxis(result, 0, 1).reshape(CH, NT).astype(jnp.bfloat16)

def whitened_spectra(decimated):
    segments = decimated.astype(jnp.float32).reshape(decimated.shape[0], NSEG, SEG)
    spectra = jnp.fft.fft(segments, n=2 * SEG, axis=-1)[..., :SEG]
    real_part = jnp.real(spectra)
    imag_part = jnp.imag(spectra)
    magnitude = jnp.sqrt(real_part * real_part + imag_part * imag_part)
    banded = magnitude.reshape(magnitude.shape[:-1] + (SEG // BAND, BAND))
    amplitude = jnp.repeat(lax.optimization_barrier(jnp.mean(banded, axis=-1)), BAND, axis=-1) + EPSILON
    return ((real_part / amplitude).astype(jnp.bfloat16), (imag_part / amplitude).astype(jnp.bfloat16))

def reference(raw, fir_taps, offsets, vs_index):
    taps_narrow = fir_taps.astype(jnp.bfloat16)
    taps_wide = lax.optimization_barrier(taps_narrow).astype(jnp.float32)
    cross_re = jnp.zeros((NVS, CH, SEG), jnp.float32)
    cross_im = jnp.zeros((NVS, CH, SEG), jnp.float32)
    for window_idx in range(NWIN):
        decimated = decimate_window(raw[window_idx], taps_wide, offsets[window_idx])
        white_re, white_im = whitened_spectra(decimated)
        own_re = white_re.astype(jnp.float32)
        own_im = white_im.astype(jnp.float32)
        source_re = own_re[vs_index]
        source_im = own_im[vs_index]
        cross_re = cross_re + jnp.einsum('cqf,sqf->scf', own_re, source_re) + jnp.einsum('cqf,sqf->scf', own_im, source_im)
        cross_im = cross_im + jnp.einsum('cqf,sqf->scf', own_im, source_re) - jnp.einsum('cqf,sqf->scf', own_re, source_im)
    scale_out = 1.0 / math.sqrt(SEG * NSEG * NWIN)

    def one_source(operands):
        part_re, part_im = operands
        padded = jnp.pad(part_re + 1j * part_im, ((0, 0), (0, SEG)))
        full = jnp.real(jnp.fft.ifft(padded, axis=-1)) * (2 * SEG)
        return jnp.concatenate([full[:, 2 * SEG - SEG // 2:], full[:, :SEG // 2]], axis=-1) * scale_out
    return lax.map(one_source, (cross_re, cross_im))
```

```python
import functools
import math

import jax
import jax.numpy as jnp
import numpy as np
from jax import lax
from jax.experimental import pallas as pl
from jax.experimental.pallas import tpu as pltpu
from jax.sharding import PartitionSpec as P

R = 10
TAPS = 64
TD = 128
SEG = 2048
BAND = 64
EPSILON = 1e-06

PH = 16
LO = 256
NA = SEG // PH
NN = SEG // LO
HALF = LO // 128
SRC_BLOCKS = 2


def transform_tables():
    a = np.arange(NA)[:, None]
    m = np.arange(LO)[None, :]
    angle = 2 * np.pi * ((a * m) % LO) / LO
    cos, sin = np.cos(angle), np.sin(angle)
    forward = np.block([[cos.T, -sin.T], [sin.T, cos.T]])
    p = np.arange(PH)[:, None]
    turn = 2 * np.pi * (p * m) / (2 * SEG)
    full = 2 * np.pi * (((PH * a[None] + p[:, :, None]) * m[None]) % (2 * SEG)) / (2 * SEG)
    fc, fs = np.cos(full), np.sin(full)
    inverse = np.concatenate(
        [np.concatenate([fc, fs], axis=2), np.concatenate([-fs, fc], axis=2)], axis=1
    )
    lane = np.arange(NA)
    per_band = BAND // PH
    band = (lane[:, None] // per_band == lane[None, :] // per_band).astype(np.float32)
    return (
        jnp.asarray(forward, jnp.bfloat16),
        jnp.asarray(inverse, jnp.bfloat16),
        jnp.asarray(np.stack([np.cos(turn), np.sin(turn)]), jnp.float32),
        jnp.asarray(band, jnp.float32),
    )


def decimate_kernel(files, wins, offset_ref, taps_ref, index_ref, raw_ref, halo_ref, out_ref):
    channels = raw_ref.shape[0]
    half = TD // 2
    stride = R * half
    width = stride + 128
    offset = offset_ref[0, 0]
    taps = jnp.broadcast_to(taps_ref[...], (half, TAPS)).astype(jnp.bfloat16)
    k = lax.broadcasted_iota(jnp.int32, (TAPS, 256), 0)
    lane = lax.broadcasted_iota(jnp.int32, (TAPS, 256), 1)
    place = jnp.where(lane == 128 - k, 1.0, 0.0).astype(jnp.bfloat16)
    band = jnp.dot(taps, place, preferred_element_type=jnp.float32)
    shift = lax.broadcasted_iota(jnp.int32, (half, 128), 0) * R + offset
    wide_shift = jnp.concatenate([shift, shift], axis=1)
    for bit in range(7):
        band = jnp.where((wide_shift >> bit) % 2 == 1, pltpu.roll(band, 1 << bit, 1), band)
    tiles = []
    for t in range(width // 128):
        low = jnp.where(shift // 128 == t, band[:, :128], 0.0)
        tiles.append(low + jnp.where(shift // 128 == t - 1, band[:, 128:], 0.0))
    rolled = jnp.concatenate(tiles, axis=1).astype(jnp.bfloat16)
    nt = (((1,), (1,)), ((), ()))
    zero = jnp.zeros((half, width), jnp.bfloat16)
    first = jnp.concatenate([rolled, zero], axis=0)
    second = jnp.concatenate([zero, rolled], axis=0)
    total = lax.dot_general(
        raw_ref[:, stride - 128 : 2 * stride], second, nt, preferred_element_type=jnp.float32
    )
    total += lax.dot_general(
        raw_ref[:, :stride], first[:, 128:], nt, preferred_element_type=jnp.float32
    )
    total += lax.dot_general(halo_ref[...], first[:, :128], nt, preferred_element_type=jnp.float32)
    decimated = total.astype(jnp.bfloat16)
    sources = index_ref.shape[1]
    row = lax.broadcasted_iota(jnp.int32, (channels, sources), 0)
    pick = jnp.where(row == index_ref[...], 1.0, 0.0).astype(jnp.bfloat16)
    chosen = lax.dot_general(
        pick, decimated, (((0,), (0,)), ((), ())), preferred_element_type=jnp.float32
    ).astype(jnp.bfloat16)
    per_win = sources // wins
    per_file = channels // files
    for file in range(files):
        for win in range(wins):
            dest = file * wins + win
            out_ref[dest, :per_win, :] = chosen[win * per_win : (win + 1) * per_win]
            out_ref[dest, per_win:, :] = decimated[file * per_file : (file + 1) * per_file]


def spread(x):
    terms = []
    for p in range(PH // 2 + 1):
        re, im = None, None
        for n in range(NN):
            angle = (p * n) % PH
            c, s = math.cos(2 * math.pi * angle / PH), -math.sin(2 * math.pi * angle / PH)
            if angle % (PH // 4):
                re = x[n] * c if re is None else re + x[n] * c
                im = x[n] * s if im is None else im + x[n] * s
            elif angle % (PH // 2):
                im = x[n] * round(s) if im is None else (im + x[n] if s > 0 else im - x[n])
            else:
                re = x[n] if re is None else (re + x[n] if c > 0 else re - x[n])
        terms.append((re, jnp.zeros_like(re) if im is None else im))
    return terms


def gather_lags(re, im):
    half = PH // 2
    even = [None] + [re[p] + re[PH - p] for p in range(1, half)]
    odd = [None] + [im[p] - im[PH - p] for p in range(1, half)]
    quarter = half // 2
    both = [None] + [even[p] + even[half - p] for p in range(1, quarter)]
    apart = [None] + [even[p] - even[half - p] for p in range(1, quarter)]
    oboth = [None] + [odd[p] + odd[half - p] for p in range(1, quarter)]
    oapart = [None] + [odd[p] - odd[half - p] for p in range(1, quarter)]
    ends = (re[0] + re[half], re[0] - re[half])
    cosines, sines = {}, {}
    for n in range(NN // 2 + 1):
        fold, total = (both, ends[0]) if n % 2 == 0 else (apart, ends[1])
        if n % 2 == 0:
            total = total + even[quarter] if (n // 2) % 2 == 0 else total - even[quarter]
        for p in range(1, quarter):
            c = math.cos(2 * math.pi * p * n / PH)
            if abs(c) > 1e-9:
                total = total + (fold[p] if c == 1.0 else -fold[p] if c == -1.0 else fold[p] * c)
        cosines[n] = total
        if n:
            ofold = oapart if n % 2 == 0 else oboth
            total = None
            if n % 2:
                total = odd[quarter] if n % 4 == 1 else -odd[quarter]
            for p in range(1, quarter):
                s = math.sin(2 * math.pi * p * n / PH)
                if abs(s) > 1e-9:
                    term = ofold[p] * s
                    total = term if total is None else total + term
            sines[n] = total
    lags = []
    for n in range(-NN // 2, NN // 2):
        if n == 0:
            lags.append(cosines[0])
        elif sines[abs(n)] is None:
            lags.append(cosines[abs(n)])
        elif n < 0:
            lags.append(cosines[-n] + sines[-n])
        else:
            lags.append(cosines[n] - sines[n])
    return lags


def correlate_kernel(
    files, wins, sources, scale,
    data_ref, forward_ref, inverse_ref, turn_ref, band_ref, out_ref,
    z_ref, w_ref, pair_ref, lag_ref,
):
    rows = data_ref.shape[1]
    segs = files * TD // SEG
    per_seg = files // segs
    block = sources // SRC_BLOCKS
    chans = rows - sources
    groups = wins * segs

    @pl.when(pl.program_id(0) == 0)
    def _():
        for win in range(wins):
            for seg in range(segs):
                base = (win * segs + seg) * rows
                for h in range(HALF):
                    x = [
                        data_ref[(seg * per_seg + HALF * n + h) * wins + win].astype(jnp.float32)
                        for n in range(NN)
                    ]
                    terms = spread(x)
                    for p in range(PH):
                        re, im = terms[p] if p <= PH // 2 else terms[PH - p]
                        if p > PH // 2:
                            im = -im
                        c = turn_ref[0, p : p + 1, 128 * h : 128 * h + 128]
                        s = turn_ref[1, p : p + 1, 128 * h : 128 * h + 128]
                        z_ref[p, base : base + rows, 128 * h : 128 * h + 128] = (
                            re * c + im * s
                        ).astype(jnp.bfloat16)
                        z_ref[p, base : base + rows, LO + 128 * h : LO + 128 * h + 128] = (
                            im * c - re * s
                        ).astype(jnp.bfloat16)
        total = jnp.zeros((groups * rows, NA), jnp.float32)
        for p in range(PH):
            spec = jnp.dot(z_ref[p], forward_ref[...], preferred_element_type=jnp.float32)
            w_ref[p] = spec
            re, im = spec[:, :NA], spec[:, NA:]
            total += jnp.sqrt(re * re + im * im)
        amplitude = (
            jnp.dot(
                total, band_ref[...], precision=lax.Precision.HIGHEST,
                preferred_element_type=jnp.float32,
            )
            * (1.0 / BAND)
            + EPSILON
        )
        gain = 1.0 / amplitude
        gain = jnp.concatenate([gain, gain], axis=1)
        for p in range(PH):
            w_ref[p] = (w_ref[p] * gain).astype(jnp.bfloat16).astype(jnp.float32)

    first = pl.program_id(0) * block

    def one_phase(p, _):
        own = [
            (
                w_ref[p, g * rows + sources : (g + 1) * rows, :NA],
                w_ref[p, g * rows + sources : (g + 1) * rows, NA:],
            )
            for g in range(groups)
        ]

        def pair(s):
            cre, cim = None, None
            for g in range(groups):
                row = w_ref[p, pl.ds(g * rows + first + s, 1), :]
                sre = jnp.broadcast_to(row[:, :NA], (chans, NA))
                sim = jnp.broadcast_to(row[:, NA:], (chans, NA))
                ore, oim = own[g]
                tre = ore * sre + oim * sim
                tim = oim * sre - ore * sim
                cre = tre if cre is None else cre + tre
                cim = tim if cim is None else cim + tim
            return cre, cim

        for s in range(0, block, 2):
            r0, i0 = pair(s)
            r1, i1 = pair(s + 1)
            pair_ref[s * chans : (s + 2) * chans, :NA] = jnp.concatenate([r0, r1], 0).astype(jnp.bfloat16)
            pair_ref[s * chans : (s + 2) * chans, NA:] = jnp.concatenate([i0, i1], 0).astype(jnp.bfloat16)
        lag_ref[p] = jnp.dot(pair_ref[...], inverse_ref[p], preferred_element_type=jnp.float32)
        return 0

    lax.fori_loop(0, PH, one_phase, 0)

    def one_source(s, _):
        at = pl.ds(pl.multiple_of(s * chans, chans), chans)
        for h in range(HALF):
            lo = 128 * h
            re = [lag_ref[p, at, lo : lo + 128] for p in range(PH)]
            im = [lag_ref[p, at, LO + lo : LO + lo + 128] for p in range(PH)]
            for n, value in enumerate(gather_lags(re, im)):
                out_ref[s, :, LO * n + lo : LO * n + lo + 128] = value * scale
        return 0

    lax.fori_loop(0, block, one_source, 0)


def local(raw, fir_taps, offsets, vs_index):
    samples = raw[0]
    channels = samples.shape[0]
    files = lax.axis_size("file")
    wins = lax.axis_size("win")
    sources = vs_index.shape[0] // wins
    chans = channels // files
    rows = sources + chans
    segs = files * TD // SEG
    halo = lax.ppermute(
        samples[:, samples.shape[1] - 128 :], "file", [(i, i + 1) for i in range(files - 1)]
    )
    vmem = pl.BlockSpec(memory_space=pltpu.VMEM)
    packed = pl.pallas_call(
        functools.partial(decimate_kernel, files, wins),
        out_shape=jax.ShapeDtypeStruct((files * wins, rows, TD), jnp.bfloat16),
        in_specs=[pl.BlockSpec(memory_space=pltpu.SMEM), vmem, vmem, vmem, vmem],
        out_specs=vmem,
        compiler_params=pltpu.CompilerParams(vmem_limit_bytes=32 * 2**20),
        name="decimate",
    )(offsets, fir_taps[None, :], vs_index[None, :], samples, halo)
    data = lax.all_to_all(packed, ("file", "win"), split_axis=0, concat_axis=0, tiled=True)
    forward, inverse, turn, band = transform_tables()
    groups = wins * segs
    block = sources // SRC_BLOCKS
    scale = 1.0 / math.sqrt(SEG * segs * wins)
    whole = lambda shape: pl.BlockSpec(shape, lambda i: (0,) * len(shape))
    return pl.pallas_call(
        functools.partial(correlate_kernel, files, wins, sources, scale),
        grid=(SRC_BLOCKS,),
        out_shape=jax.ShapeDtypeStruct((sources, chans, SEG), jnp.float32),
        in_specs=[whole(x.shape) for x in (data, forward, inverse, turn, band)],
        out_specs=pl.BlockSpec((block, chans, SEG), lambda i: (i, 0, 0)),
        scratch_shapes=[
            pltpu.VMEM((PH, groups * rows, 2 * LO), jnp.bfloat16),
            pltpu.VMEM((PH, groups * rows, 2 * NA), jnp.float32),
            pltpu.VMEM((block * chans, 2 * NA), jnp.bfloat16),
            pltpu.VMEM((PH, block * chans, 2 * LO), jnp.float32),
        ],
        compiler_params=pltpu.CompilerParams(vmem_limit_bytes=56 * 2**20),
        name="correlate",
    )(data, forward, inverse, turn, band)


def solution(mesh):
    return jax.shard_map(
        local,
        mesh=mesh,
        in_specs=(P("win", None, "file"), P(), P("win", "file"), P()),
        out_specs=P("win", "file", None),
        check_vma=False,
    )
```

```python
import functools
import math

import jax
import jax.numpy as jnp
import numpy as np
from jax import lax
from jax.experimental import pallas as pl
from jax.experimental.pallas import tpu as pltpu
from jax.sharding import PartitionSpec as P

R = 10
TAPS = 64
TD = 128
SEG = 2048
BAND = 64
EPSILON = 1e-06

PH = 16
LO = 256
NA = SEG // PH
NN = SEG // LO
HALF = LO // 128
PAIRS = PH // 2
EARLY = 8
GROUP = 4

NT = (((1,), (1,)), ((), ()))
NN_DIMS = (((1,), (0,)), ((), ()))
F32 = jnp.float32
BF16 = jnp.bfloat16


def split_table(x):
    high = x.astype(BF16)
    return np.stack([high, (x - high.astype(np.float64)).astype(BF16)])


def transform_table():
    a = np.arange(NA)[:, None]
    m = np.arange(LO)[None, :]

    def wave(f):
        angle = 2 * np.pi * ((f * m) % (2 * SEG)) / (2 * SEG)
        return np.cos(angle), np.sin(angle)

    c, s = wave(PH * a)
    cc, ss = wave(PH * (a + 1))
    folded = np.block([[c, s], [-s, c], [cc, -ss], [-ss, -cc]])
    c8, s8 = wave(PH * a + PH // 2)
    z = np.zeros_like(c)
    ends = np.block([[c, z], [-s, z], [z, c8], [z, -s8]])
    return jnp.asarray(split_table(np.stack([ends, folded])))


def three_pass(high, low, table_high, table_low, dims):
    dot = functools.partial(lax.dot_general, dimension_numbers=dims, preferred_element_type=F32)
    return dot(high, table_high) + (dot(low, table_high) + dot(high, table_low))


def split(x):
    high = x.astype(BF16)
    return high, (x - high.astype(F32)).astype(BF16)


def decimate_kernel(
    files, wins,
    offset_hbm, taps_hbm, index_hbm, raw_hbm, out_ref,
    offset_ref, taps_ref, index_ref, raw_ref, sems,
):
    copies = [
        pltpu.make_async_copy(source, target, sems.at[i])
        for i, (source, target) in enumerate(
            (
                (offset_hbm, offset_ref),
                (taps_hbm, taps_ref),
                (index_hbm, index_ref),
                (raw_hbm, raw_ref),
            )
        )
    ]
    for copy in copies:
        copy.start()
    channels, samples = raw_ref.shape
    half = TD // 2
    stride = R * half
    width = stride + 128
    copies[0].wait()
    copies[1].wait()
    offset = offset_ref[0, 0]
    taps = jnp.broadcast_to(taps_ref[...], (half, TAPS)).astype(BF16)
    k = lax.broadcasted_iota(jnp.int32, (TAPS, 256), 0)
    lane = lax.broadcasted_iota(jnp.int32, (TAPS, 256), 1)
    place = jnp.where(lane == 128 - k, 1.0, 0.0).astype(BF16)
    band = jnp.dot(taps, place, preferred_element_type=F32)
    shift = lax.broadcasted_iota(jnp.int32, (half, 128), 0) * R + offset
    wide_shift = jnp.concatenate([shift, shift], axis=1)
    for bit in range(7):
        band = jnp.where((wide_shift >> bit) % 2 == 1, pltpu.roll(band, 1 << bit, 1), band)
    tiles = []
    for t in range(width // 128):
        low = jnp.where(shift // 128 == t, band[:, :128], 0.0)
        tiles.append(low + jnp.where(shift // 128 == t - 1, band[:, 128:], 0.0))
    rolled = jnp.concatenate(tiles, axis=1).astype(BF16)
    zero = jnp.zeros((half, width), BF16)
    first = jnp.concatenate([rolled, zero], axis=0)
    second = jnp.concatenate([zero, rolled], axis=0)
    copies[2].wait()
    sources = index_ref.shape[1]
    row = lax.broadcasted_iota(jnp.int32, (channels, sources), 0)
    pick = jnp.where(row == index_ref[...], 1.0, 0.0).astype(BF16)
    copies[3].wait()
    total = lax.dot_general(
        raw_ref[:, stride - 128 : 2 * stride], second, NT, preferred_element_type=F32
    )
    total += lax.dot_general(raw_ref[:, :stride], first[:, 128:], NT, preferred_element_type=F32)
    decimated = total.astype(BF16)
    lane = lax.broadcasted_iota(jnp.int32, (channels, 128), 1)
    low = jnp.where(lane < EARLY, total - decimated.astype(F32), 0.0)
    tail = raw_ref[:, samples - 128 :].astype(F32)
    tail = jnp.where(lane == TAPS, offset.astype(F32), tail)
    everything = jnp.concatenate([decimated, tail.astype(BF16), low.astype(BF16)], axis=1)
    chosen = lax.dot_general(
        pick, everything, (((0,), (0,)), ((), ())), preferred_element_type=F32
    )
    per_win = sources // wins
    share = per_win // 2
    per_file = channels // files
    lower = lane[:per_file] < 64

    def low_lanes(value, i):
        return pltpu.roll(value, 64 + EARLY * i, 1)

    wide = jnp.concatenate([taps_ref[...], jnp.zeros((1, 128 - TAPS), F32)], axis=1)
    row = lax.broadcasted_iota(jnp.int32, (per_file, 128), 0)
    carried = jnp.where(row == 0, pltpu.roll(wide, 96, 1), pltpu.roll(wide, 64, 1))
    carried = jnp.where((row < 2) & (lane[:per_file] >= 96), carried, 0.0)
    blocks = {}
    for win in range(wins):
        for core in range(2):
            at = win * per_win + core * share
            part = chosen[at : at + share]
            tails = pltpu.roll(part[:, 128:256], 64, 1)
            lows = part[:, 256:]
            packed = carried + low_lanes(lows[:per_file], 0)
            for i in range(1, share // per_file):
                packed += low_lanes(lows[i * per_file : (i + 1) * per_file], i)
            second = tails[per_file:] if share > per_file else jnp.zeros_like(packed)
            blocks[win, core] = (
                part[:, :128].astype(BF16), tails[:per_file], jnp.where(lower, second, packed)
            )
    for file in range(files):
        own = slice(file * per_file, (file + 1) * per_file)
        own_low = low_lanes(low[own], share // per_file)
        for win in range(wins):
            dest = file * wins + win
            dec, tails, packed = blocks[win, file % 2]
            out_ref[dest, : 2 * per_file, :] = jnp.concatenate(
                [jnp.where(lower, tails, tail[own]), packed + own_low], axis=0
            ).astype(BF16)
            out_ref[dest, 2 * per_file : 2 * per_file + share, :] = dec
            out_ref[dest, 2 * per_file + share :, :] = decimated[own]


def spread(x):
    terms = []
    for p in range(PH // 2 + 1):
        re, im = None, None
        for n in range(NN):
            angle = (p * n) % PH
            c, s = math.cos(2 * math.pi * angle / PH), -math.sin(2 * math.pi * angle / PH)
            if angle % (PH // 4):
                re = x[n] * c if re is None else re + x[n] * c
                im = x[n] * s if im is None else im + x[n] * s
            elif angle % (PH // 2):
                im = x[n] * round(s) if im is None else (im + x[n] if s > 0 else im - x[n])
            else:
                re = x[n] if re is None else (re + x[n] if c > 0 else re - x[n])
        terms.append((re, im))
    return terms


def forward_kernel(
    files, wins, chans, scale,
    data_ref, table_hbm, own_ref, src_ref, table_ref, turn_ref,
    rest_ref, fixed_ref, high_ref, low_ref, spec_ref, sems,
):
    copies = [
        pltpu.make_async_copy(source, target, sems.at[i])
        for i, (source, target) in enumerate(
            ((table_hbm.at[0], table_ref), (table_hbm.at[1], rest_ref))
        )
    ]
    for copy in copies:
        copy.start()
    phase = lax.broadcasted_iota(jnp.int32, (8, LO), 0) * lax.broadcasted_iota(jnp.int32, (8, LO), 1)
    angle = phase.astype(F32) * (math.pi / SEG)
    turns = (jnp.cos(angle), jnp.sin(angle))
    for p in range(PAIRS):
        for i in range(2):
            turn_ref[i, p] = jnp.broadcast_to(turns[i][p : p + 1], (8, LO))
    rows = fixed_ref.shape[1]
    share = rows - chans
    lead = 2 * chans
    segs = files * TD // SEG
    per_seg = files // segs
    devices = files * wins

    first = data_ref[0, chans : 2 * chans, :].astype(F32)
    row = lax.broadcasted_iota(jnp.int32, (TAPS, 128), 0)
    lane = lax.broadcasted_iota(jnp.int32, (TAPS, 128), 1)
    taps = jnp.where(lane[:1] < 32, pltpu.roll(first[:1], 32, 1), pltpu.roll(first[1:2], 64, 1))
    share_of = jnp.where(lane < TAPS, jnp.broadcast_to(taps, (TAPS, 128)), 0.0)
    for bit in range(6):
        move = (TAPS - row) >> bit
        share_of = jnp.where(move % 2 == 1, pltpu.roll(share_of, 128 - (1 << bit), 1), share_of)
    share_of = jnp.where((lane < row) & (row > 0), share_of, 0.0).astype(BF16)
    nothing = jnp.zeros((TAPS, 128), BF16)
    row = lax.broadcasted_iota(jnp.int32, (128, 128), 0)
    lane = lax.broadcasted_iota(jnp.int32, (128, 128), 1)
    columns = [
        jnp.concatenate([share_of, nothing], axis=0),
        jnp.concatenate([nothing, share_of], axis=0),
        jnp.where(row == 0, 1.0, 0.0).astype(BF16),
    ]
    for i in range(rows // chans):
        columns.append(
            jnp.where((row == 64 + EARLY * i + lane) & (lane < EARLY), 1.0, 0.0).astype(BF16)
        )
    collapse = jnp.where((row // R == lane) & (lane < EARLY), 1.0, 0.0).astype(BF16)
    tails = data_ref[:, :lead, :].reshape(devices * lead, 128)
    mixed = jnp.dot(tails, jnp.concatenate(columns, axis=1), preferred_element_type=F32)
    mixed = mixed.reshape(devices, lead, len(columns) * 128)
    residue = (lax.broadcasted_iota(jnp.int32, (1, 1, 128), 2) % R).astype(F32)
    offset = mixed[wins:, :, 256:384]

    def early(value, kept):
        value = jnp.where(residue == offset[:, :kept], value[:-wins, :kept], 0.0)
        value = value.reshape((devices - wins) * kept, 128)
        high, low = split(value)
        value = jnp.dot(high, collapse, preferred_element_type=F32) + jnp.dot(
            low, collapse, preferred_element_type=F32
        )
        value = value.reshape(devices - wins, kept, 128)
        return jnp.concatenate([jnp.zeros((wins, kept, 128), F32), value], axis=0)

    added = jnp.concatenate(
        [early(mixed[:, :, :128], share), early(mixed[:, :, 128:256], chans)], axis=1
    )
    lows = jnp.concatenate(
        [
            mixed[:, chans:, 128 * (3 + i) : 128 * (4 + i)]
            for i in range(rows // chans)
        ],
        axis=1,
    )
    fixed_ref[...] = (data_ref[:, lead:, :].astype(F32) + (lows + added)).astype(BF16).astype(F32)

    for win in range(wins):
        for seg in range(segs):
            base = (win * segs + seg) * rows
            for h in range(HALF):
                x = [fixed_ref[(seg * per_seg + HALF * n + h) * wins + win] for n in range(NN)]
                terms = spread(x)
                for p in range(PAIRS):
                    if p:
                        re, im = terms[p]
                        c = turn_ref[0, p, :1, 128 * h : 128 * h + 128]
                        s = turn_ref[1, p, :1, 128 * h : 128 * h + 128]
                        re, im = re * c + im * s, im * c - re * s
                    else:
                        re, im = terms[0][0], terms[PAIRS][0]
                    for part, value in enumerate((re, im)):
                        at = slice(LO * part + 128 * h, LO * part + 128 * h + 128)
                        high, low = split(value)
                        high_ref[p, base : base + rows, at] = high
                        low_ref[p, base : base + rows, at] = low
    groups = wins * segs
    count = groups * rows
    for copy in copies:
        copy.wait()
    spec_ref[0] = three_pass(high_ref[0], low_ref[0], table_ref[0], rest_ref[0], NT)
    spec_ref[1:] = three_pass(
        high_ref[1:].reshape((PAIRS - 1) * count, 2 * LO),
        low_ref[1:].reshape((PAIRS - 1) * count, 2 * LO),
        table_ref[1],
        rest_ref[1],
        NT,
    ).reshape(PAIRS - 1, count, 4 * NA)
    total = jnp.zeros((count, NA), F32)
    for p in range(PAIRS):
        for part in range(2):
            re = spec_ref[p, :, 2 * NA * part : 2 * NA * part + NA]
            im = spec_ref[p, :, 2 * NA * part + NA : 2 * NA * part + 2 * NA]
            total += jnp.sqrt(re * re + im * im)
    high, low = split(total)
    low2 = (total - high.astype(F32) - low.astype(F32)).astype(BF16)
    row = lax.broadcasted_iota(jnp.int32, (NA, NA), 0)
    lane = lax.broadcasted_iota(jnp.int32, (NA, NA), 1)
    per_band = BAND // PH
    band = jnp.where(row // per_band == lane // per_band, 1.0, 0.0).astype(BF16)
    amplitude = (
        jnp.dot(high, band, preferred_element_type=F32)
        + jnp.dot(low, band, preferred_element_type=F32)
        + jnp.dot(low2, band, preferred_element_type=F32)
    ) * (1.0 / BAND) + EPSILON
    gain = 1.0 / amplitude
    gain = jnp.concatenate([gain] * 4, axis=1)
    for p in range(PAIRS):
        white = (spec_ref[p] * gain).astype(BF16)
        for group in range(groups):
            src_ref[p, group] = white[group * rows : group * rows + share]
            own_ref[p, group] = white[group * rows + share : (group + 1) * rows].astype(F32) * scale


def gather_lags(ends, re, im):
    half = PH // 2
    quarter = half // 2
    both = [None] + [re[p] + re[half - p] for p in range(1, quarter)]
    apart = [None] + [re[p] - re[half - p] for p in range(1, quarter)]
    oboth = [None] + [im[p] + im[half - p] for p in range(1, quarter)]
    oapart = [None] + [im[p] - im[half - p] for p in range(1, quarter)]
    edge = (ends[0] + ends[1], ends[0] - ends[1])
    cosines, sines = {}, {}
    for n in range(NN // 2 + 1):
        fold, total = (both, edge[0]) if n % 2 == 0 else (apart, edge[1])
        if n % 2 == 0:
            total = total + re[quarter] if (n // 2) % 2 == 0 else total - re[quarter]
        for p in range(1, quarter):
            c = math.cos(2 * math.pi * p * n / PH)
            if abs(abs(c) - 1) < 1e-9:
                total = total + fold[p] if c > 0 else total - fold[p]
            elif abs(c) > 1e-9:
                total = total + fold[p] * c
        cosines[n] = total
        if n:
            ofold = oapart if n % 2 == 0 else oboth
            total = None
            for p in range(1, quarter):
                s = math.sin(2 * math.pi * p * n / PH)
                if abs(s) > 1e-9:
                    term = ofold[p] if abs(s - 1) < 1e-9 else -ofold[p] if abs(s + 1) < 1e-9 else ofold[p] * s
                    total = term if total is None else total + term
            if n % 2:
                total = total + im[quarter] if n % 4 == 1 else total - im[quarter]
            sines[n] = total
    lags = []
    for n in range(-NN // 2, NN // 2):
        if n == 0:
            lags.append(cosines[0])
        else:
            lags.append(cosines[-n] + sines[-n] if n < 0 else cosines[n] - sines[n])
    return lags


def pair_kernel(mine, own_ref, src_ref, table_ref, turn_ref, *refs):
    out_hbm, wide_ref, pair_a, pair_b, lag_a, lag_b, out_ref, sems = refs[-8:]
    groups, chans = own_ref.shape[1:3]
    share = src_ref.shape[2]
    wide_ref[...] = src_ref[...].astype(F32)
    size = GROUP * chans
    core = lax.axis_index("file") % 2
    place = (core if mine else 1 - core) * share

    def written(i):
        return pltpu.make_async_copy(
            out_ref.at[pl.ds(i * GROUP, GROUP)],
            out_hbm.at[pl.ds(place + i * GROUP, GROUP)],
            sems.at[i],
        )

    def cross(first, pair_ref):
        for p in range(PAIRS):
            for part in range(2):
                left = 2 * NA * part
                own = [
                    (own_ref[p, g, :, left : left + NA], own_ref[p, g, :, left + NA : left + 2 * NA])
                    for g in range(groups)
                ]
                for s in range(0, GROUP, 2):
                    res, ims = [], []
                    for one in range(2):
                        cre, cim = None, None
                        for g in range(groups):
                            at = first + s + one
                            sre = wide_ref[p, g, at : at + 1, left : left + NA]
                            sim = wide_ref[p, g, at : at + 1, left + NA : left + 2 * NA]
                            ore, oim = own[g]
                            tre = ore * sre + oim * sim
                            tim = oim * sre - ore * sim
                            cre = tre if cre is None else cre + tre
                            cim = tim if cim is None else cim + tim
                        res.append(cre)
                        ims.append(cim)
                    at = slice(s * chans, (s + 2) * chans)
                    pair_ref[p, at, left : left + NA] = jnp.concatenate(res, 0).astype(BF16)
                    pair_ref[p, at, left + NA : left + 2 * NA] = jnp.concatenate(ims, 0).astype(BF16)

    def product(pair_ref, lag_ref):
        lag_ref[0] = jnp.dot(pair_ref[0], table_ref[0], preferred_element_type=F32)
        lag_ref[1:] = jnp.dot(
            pair_ref[1:].reshape((PAIRS - 1) * size, 4 * NA),
            table_ref[1],
            preferred_element_type=F32,
        ).reshape(PAIRS - 1, size, 2 * LO)

    def lags(first, lag_ref):
        for s in range(GROUP):
            at = slice(s * chans, (s + 1) * chans)
            for h in range(HALF):
                lo = 128 * h
                ends = [lag_ref[0, at, LO * i + lo : LO * i + lo + 128] for i in range(2)]
                re, im = [None], [None]
                for p in range(1, PAIRS):
                    u = lag_ref[p, at, lo : lo + 128]
                    v = lag_ref[p, at, LO + lo : LO + lo + 128]
                    c = turn_ref[0, p, :, lo : lo + 128]
                    d = turn_ref[1, p, :, lo : lo + 128]
                    re.append(c * u - d * v)
                    im.append(c * v + d * u)
                for n, value in enumerate(gather_lags(ends, re, im)):
                    out_ref[first + s, :, LO * n + lo : LO * n + lo + 128] = value

    steps = share // GROUP
    pairs, lagged = (pair_a, pair_b), (lag_a, lag_b)
    cross(0, pair_a)
    for i in range(steps):
        product(pairs[i % 2], lagged[i % 2])
        if i + 1 < steps:
            cross((i + 1) * GROUP, pairs[(i + 1) % 2])
        if i:
            lags((i - 1) * GROUP, lagged[(i - 1) % 2])
            written(i - 1).start()
    lags((steps - 1) * GROUP, lagged[(steps - 1) % 2])
    written(steps - 1).start()
    for i in range(steps):
        written(i).wait()


def pair_call(mine, own, src, table, turn, sources, done=None):
    groups, chans = own.shape[1:3]
    share = src.shape[2]
    vmem = pl.BlockSpec(memory_space=pltpu.VMEM)
    hbm = pl.BlockSpec(memory_space=pltpu.HBM)
    operands = [own, src, table, turn]
    specs = [vmem] * 4
    aliases = {}
    if done is not None:
        aliases = {len(operands): 0}
        operands.append(done)
        specs.append(hbm)
    return pl.pallas_call(
        functools.partial(pair_kernel, mine),
        in_specs=specs,
        out_specs=hbm,
        scratch_shapes=[
            pltpu.VMEM((PAIRS, groups, share, 4 * NA), F32),
            pltpu.VMEM((PAIRS, GROUP * chans, 4 * NA), BF16),
            pltpu.VMEM((PAIRS, GROUP * chans, 4 * NA), BF16),
            pltpu.VMEM((PAIRS, GROUP * chans, 2 * LO), F32),
            pltpu.VMEM((PAIRS, GROUP * chans, 2 * LO), F32),
            pltpu.VMEM((share, chans, SEG), F32),
            pltpu.SemaphoreType.DMA((share // GROUP,)),
        ],
        out_shape=jax.ShapeDtypeStruct((sources, chans, SEG), F32),
        input_output_aliases=aliases,
        compiler_params=pltpu.CompilerParams(vmem_limit_bytes=32 * 2**20),
        name="pair",
    )(*operands)


def local(raw, fir_taps, offsets, vs_index):
    samples = raw[0]
    channels = samples.shape[0]
    files = lax.axis_size("file")
    wins = lax.axis_size("win")
    sources = vs_index.shape[0] // wins
    share = sources // 2
    chans = channels // files
    rows = share + chans
    segs = files * TD // SEG
    groups = wins * segs
    taps = fir_taps[None, :]
    index = vs_index[None, :]
    table = transform_table()
    scale = 1.0 / math.sqrt(SEG * segs * wins)
    hbm = pl.BlockSpec(memory_space=pltpu.HBM)
    vmem = pl.BlockSpec(memory_space=pltpu.VMEM)
    packed = pl.pallas_call(
        functools.partial(decimate_kernel, files, wins),
        out_shape=jax.ShapeDtypeStruct((files * wins, 2 * chans + rows, TD), BF16),
        in_specs=[hbm] * 4,
        out_specs=vmem,
        scratch_shapes=[
            pltpu.SMEM(offsets.shape, jnp.int32),
            pltpu.VMEM(taps.shape, F32),
            pltpu.VMEM(index.shape, jnp.int32),
            pltpu.VMEM(samples.shape, BF16),
            pltpu.SemaphoreType.DMA((4,)),
        ],
        compiler_params=pltpu.CompilerParams(vmem_limit_bytes=60 * 2**20),
        name="decimate",
    )(offsets, taps, index, samples)
    data = lax.all_to_all(packed, ("file", "win"), split_axis=0, concat_axis=0, tiled=True)
    own, src, table_high, turn = pl.pallas_call(
        functools.partial(forward_kernel, files, wins, chans, scale),
        out_shape=(
            jax.ShapeDtypeStruct((PAIRS, groups, chans, 4 * NA), F32),
            jax.ShapeDtypeStruct((PAIRS, groups, share, 4 * NA), BF16),
            jax.ShapeDtypeStruct(table.shape[1:], BF16),
            jax.ShapeDtypeStruct((2, PAIRS, 8, LO), F32),
        ),
        in_specs=[vmem, hbm],
        out_specs=(vmem, vmem, vmem, vmem),
        scratch_shapes=[
            pltpu.VMEM(table.shape[1:], BF16),
            pltpu.VMEM((files * wins, rows, TD), F32),
            pltpu.VMEM((PAIRS, groups * rows, 2 * LO), BF16),
            pltpu.VMEM((PAIRS, groups * rows, 2 * LO), BF16),
            pltpu.VMEM((PAIRS, groups * rows, 4 * NA), F32),
            pltpu.SemaphoreType.DMA((2,)),
        ],
        compiler_params=pltpu.CompilerParams(vmem_limit_bytes=103 * 2**19),
        name="forward",
    )(data, table)
    other = lax.ppermute(src, "file", [(i, i ^ 1) for i in range(files)])
    half = pair_call(True, own, src, table_high, turn, sources)
    return pair_call(False, own, other, table_high, turn, sources, half)


def solution(mesh):
    return jax.shard_map(
        local,
        mesh=mesh,
        in_specs=(P("win", None, "file"), P(), P("win", "file"), P()),
        out_specs=P("win", "file", None),
        check_vma=False,
    )
```

```python
import functools
import math

import jax
import jax.numpy as jnp
import numpy as np
from jax import lax
from jax.experimental import pallas as pl
from jax.experimental.pallas import tpu as pltpu
from jax.sharding import PartitionSpec as P

R = 10
TAPS = 64
TD = 128
SEG = 2048
BAND = 64
EPSILON = 1e-06

PH = 16
LO = 256
NA = SEG // PH
NN = SEG // LO
HALF = LO // 128
PAIRS = PH // 2
EARLY = 8
GROUPS = (8, 4)
TABLE_ROWS = 2048

NT = (((1,), (1,)), ((), ()))
NN_DIMS = (((1,), (0,)), ((), ()))
F32 = jnp.float32
BF16 = jnp.bfloat16


def transform_table():
    a = np.arange(NA)[:, None]
    m = np.arange(LO)[None, :]

    def wave(f):
        angle = 2 * np.pi * ((f * m) % (2 * SEG)) / (2 * SEG)
        return np.cos(angle), np.sin(angle)

    c, s = wave(PH * a)
    cc, ss = wave(PH * (a + 1))
    folded = np.block([[c, s], [-s, c], [cc, -ss], [-ss, -cc]])
    c8, s8 = wave(PH * a + PH // 2)
    z = np.zeros_like(c)
    ends = np.block([[c, z], [-s, z], [z, c8], [z, -s8]])
    waves = np.concatenate([c, s, cc, ss, c8, s8])
    high = waves.astype(BF16)
    low = (waves - high.astype(np.float64)).astype(BF16)
    inverse = np.concatenate([ends, folded]).astype(BF16)
    parts = [inverse, np.concatenate([high, low], axis=1)]
    spare = TABLE_ROWS - sum(len(part) for part in parts)
    return jnp.asarray(np.concatenate(parts + [np.zeros((spare, 2 * LO), BF16)]))


def three_pass(high, low, table_high, table_low, dims):
    dot = functools.partial(lax.dot_general, dimension_numbers=dims, preferred_element_type=F32)
    return dot(high, table_high) + (dot(low, table_high) + dot(high, table_low))


def split(x):
    high = x.astype(BF16)
    return high, (x - high.astype(F32)).astype(BF16)


def decimate_kernel(
    files, wins,
    offset_hbm, taps_hbm, index_hbm, raw_hbm, out_ref,
    offset_ref, taps_ref, index_ref, raw_ref, sems,
):
    copies = [
        pltpu.make_async_copy(source, target, sems.at[i])
        for i, (source, target) in enumerate(
            (
                (offset_hbm, offset_ref),
                (taps_hbm, taps_ref),
                (index_hbm, index_ref),
                (raw_hbm, raw_ref),
            )
        )
    ]
    for copy in copies:
        copy.start()
    channels, samples = raw_ref.shape
    half = TD // 2
    stride = R * half
    width = stride + 128
    copies[0].wait()
    copies[1].wait()
    offset = offset_ref[0, 0]
    taps = jnp.broadcast_to(taps_ref[...], (half, TAPS)).astype(BF16)
    k = lax.broadcasted_iota(jnp.int32, (TAPS, 256), 0)
    lane = lax.broadcasted_iota(jnp.int32, (TAPS, 256), 1)
    place = jnp.where(lane == 128 - k, 1.0, 0.0).astype(BF16)
    band = jnp.dot(taps, place, preferred_element_type=F32)
    band = pltpu.roll(band[:8], offset, 1)
    row = lax.broadcasted_iota(jnp.int32, (8, 256), 0)
    for bit in range(3):
        band = jnp.where((row >> bit) % 2 == 1, pltpu.roll(band, R << bit, 1), band)
    band = jnp.concatenate([band, jnp.zeros((8, width - 256), F32)], axis=1)
    tiles = [band if not i else pltpu.roll(band, 8 * R * i, 1) for i in range(half // 8)]
    rolled = jnp.concatenate(tiles, axis=0).astype(BF16)
    zero = jnp.zeros((half, width), BF16)
    first = jnp.concatenate([rolled, zero], axis=0)
    second = jnp.concatenate([zero, rolled], axis=0)
    copies[2].wait()
    sources = index_ref.shape[1]
    row = lax.broadcasted_iota(jnp.int32, (channels, sources), 0)
    pick = jnp.where(row == index_ref[...], 1.0, 0.0).astype(BF16)
    copies[3].wait()
    total = lax.dot_general(
        raw_ref[:, stride - 128 : 2 * stride], second, NT, preferred_element_type=F32
    )
    total += lax.dot_general(raw_ref[:, :stride], first[:, 128:], NT, preferred_element_type=F32)
    decimated = total.astype(BF16)
    lane = lax.broadcasted_iota(jnp.int32, (channels, 128), 1)
    low = jnp.where(lane < EARLY, total - decimated.astype(F32), 0.0)
    tail = raw_ref[:, samples - 128 :].astype(F32)
    tail = jnp.where(lane == TAPS, offset.astype(F32), tail)
    everything = jnp.concatenate([decimated, tail.astype(BF16), low.astype(BF16)], axis=1)
    chosen = lax.dot_general(
        pick, everything, (((0,), (0,)), ((), ())), preferred_element_type=F32
    )
    per_win = sources // wins
    share = per_win // 2
    per_file = channels // files
    lower = lane[:per_file] < 64

    def low_lanes(value, i):
        return pltpu.roll(value, 64 + EARLY * i, 1)

    wide = jnp.concatenate([taps_ref[...], jnp.zeros((1, 128 - TAPS), F32)], axis=1)
    row = lax.broadcasted_iota(jnp.int32, (per_file, 128), 0)
    carried = jnp.where(row == 0, pltpu.roll(wide, 96, 1), pltpu.roll(wide, 64, 1))
    carried = jnp.where((row < 2) & (lane[:per_file] >= 96), carried, 0.0)
    blocks = {}
    for win in range(wins):
        for core in range(2):
            at = win * per_win + core * share
            part = chosen[at : at + share]
            tails = pltpu.roll(part[:, 128:256], 64, 1)
            lows = part[:, 256:]
            packed = carried + low_lanes(lows[:per_file], 0)
            for i in range(1, share // per_file):
                packed += low_lanes(lows[i * per_file : (i + 1) * per_file], i)
            second = tails[per_file:] if share > per_file else jnp.zeros_like(packed)
            blocks[win, core] = (
                part[:, :128].astype(BF16), tails[:per_file], jnp.where(lower, second, packed)
            )
    for file in range(files):
        own = slice(file * per_file, (file + 1) * per_file)
        own_low = low_lanes(low[own], share // per_file)
        for win in range(wins):
            dest = file * wins + win
            dec, tails, packed = blocks[win, file % 2]
            out_ref[dest, : 2 * per_file, :] = jnp.concatenate(
                [jnp.where(lower, tails, tail[own]), packed + own_low], axis=0
            ).astype(BF16)
            out_ref[dest, 2 * per_file : 2 * per_file + share, :] = dec
            out_ref[dest, 2 * per_file + share :, :] = decimated[own]


def spread(x):
    terms = []
    for p in range(PH // 2 + 1):
        re, im = None, None
        for n in range(NN):
            angle = (p * n) % PH
            c, s = math.cos(2 * math.pi * angle / PH), -math.sin(2 * math.pi * angle / PH)
            if angle % (PH // 4):
                re = x[n] * c if re is None else re + x[n] * c
                im = x[n] * s if im is None else im + x[n] * s
            elif angle % (PH // 2):
                im = x[n] * round(s) if im is None else (im + x[n] if s > 0 else im - x[n])
            else:
                re = x[n] if re is None else (re + x[n] if c > 0 else re - x[n])
        terms.append((re, im))
    return terms


def forward_kernel(
    files, wins, chans, scale,
    data_ref, table_hbm, own_ref, src_ref, table_ref, turn_ref,
    waves_ref, fixed_ref, high_ref, low_ref, spec_ref, sems,
):
    copies = [
        pltpu.make_async_copy(source, target, sems.at[i])
        for i, (source, target) in enumerate(
            (
                (table_hbm.at[pl.ds(8 * NA, 6 * NA)], waves_ref),
                (table_hbm.at[pl.ds(0, 8 * NA)], table_ref),
            )
        )
    ]
    copies[0].start()
    phase = lax.broadcasted_iota(jnp.int32, (8, LO), 0) * lax.broadcasted_iota(jnp.int32, (8, LO), 1)
    angle = phase.astype(F32) * (math.pi / SEG)
    turns = (jnp.cos(angle), jnp.sin(angle))
    for p in range(PAIRS):
        for i in range(2):
            turn_ref[i, p] = jnp.broadcast_to(turns[i][p : p + 1], (8, LO))
    rows = fixed_ref.shape[1]
    share = rows - chans
    lead = 2 * chans
    segs = files * TD // SEG
    per_seg = files // segs
    devices = files * wins

    first = data_ref[0, chans : 2 * chans, :].astype(F32)
    row = lax.broadcasted_iota(jnp.int32, (TAPS, 128), 0)
    lane = lax.broadcasted_iota(jnp.int32, (TAPS, 128), 1)
    taps = jnp.where(lane[:1] < 32, pltpu.roll(first[:1], 32, 1), pltpu.roll(first[1:2], 64, 1))
    share_of = jnp.where(lane < TAPS, jnp.broadcast_to(taps, (TAPS, 128)), 0.0)
    for bit in range(6):
        move = (TAPS - row) >> bit
        share_of = jnp.where(move % 2 == 1, pltpu.roll(share_of, 128 - (1 << bit), 1), share_of)
    share_of = jnp.where((lane < row) & (row > 0), share_of, 0.0).astype(BF16)
    nothing = jnp.zeros((TAPS, 128), BF16)
    row = lax.broadcasted_iota(jnp.int32, (128, 128), 0)
    lane = lax.broadcasted_iota(jnp.int32, (128, 128), 1)
    columns = [
        jnp.concatenate([share_of, nothing], axis=0),
        jnp.concatenate([nothing, share_of], axis=0),
        jnp.where(row == 0, 1.0, 0.0).astype(BF16),
    ]
    for i in range(rows // chans):
        columns.append(
            jnp.where((row == 64 + EARLY * i + lane) & (lane < EARLY), 1.0, 0.0).astype(BF16)
        )
    collapse = jnp.where((row // R == lane) & (lane < EARLY), 1.0, 0.0).astype(BF16)
    tails = data_ref[:, :lead, :].reshape(devices * lead, 128)
    mixed = jnp.dot(tails, jnp.concatenate(columns, axis=1), preferred_element_type=F32)
    mixed = mixed.reshape(devices, lead, len(columns) * 128)
    residue = (lax.broadcasted_iota(jnp.int32, (1, 1, 128), 2) % R).astype(F32)
    offset = mixed[wins:, :, 256:384]

    def early(value, kept):
        value = jnp.where(residue == offset[:, :kept], value[:-wins, :kept], 0.0)
        value = value.reshape((devices - wins) * kept, 128)
        high, low = split(value)
        value = jnp.dot(high, collapse, preferred_element_type=F32) + jnp.dot(
            low, collapse, preferred_element_type=F32
        )
        value = value.reshape(devices - wins, kept, 128)
        return jnp.concatenate([jnp.zeros((wins, kept, 128), F32), value], axis=0)

    added = jnp.concatenate(
        [early(mixed[:, :, :128], share), early(mixed[:, :, 128:256], chans)], axis=1
    )
    lows = jnp.concatenate(
        [
            mixed[:, chans:, 128 * (3 + i) : 128 * (4 + i)]
            for i in range(rows // chans)
        ],
        axis=1,
    )
    fixed_ref[...] = (data_ref[:, lead:, :].astype(F32) + (lows + added)).astype(BF16).astype(F32)

    for win in range(wins):
        for seg in range(segs):
            base = (win * segs + seg) * rows
            for h in range(HALF):
                x = [fixed_ref[(seg * per_seg + HALF * n + h) * wins + win] for n in range(NN)]
                terms = spread(x)
                for p in range(PAIRS):
                    if p:
                        re, im = terms[p]
                        c = turn_ref[0, p, :1, 128 * h : 128 * h + 128]
                        s = turn_ref[1, p, :1, 128 * h : 128 * h + 128]
                        re, im = re * c + im * s, im * c - re * s
                    else:
                        re, im = terms[0][0], terms[PAIRS][0]
                    for part, value in enumerate((re, im)):
                        at = slice(128 * h, 128 * h + 128)
                        high, low = split(value)
                        high_ref[part, p, base : base + rows, at] = high
                        low_ref[part, p, base : base + rows, at] = low
    groups = wins * segs
    count = groups * rows
    copies[0].wait()
    copies[1].start()

    def product(part, first, last, begin, end):
        lines = (last - first) * count
        return three_pass(
            high_ref[part, first:last].reshape(lines, LO),
            low_ref[part, first:last].reshape(lines, LO),
            waves_ref[begin * NA : end * NA, :LO],
            waves_ref[begin * NA : end * NA, LO:],
            NT,
        ).reshape(last - first, count, (end - begin) * NA)

    for part, begin in enumerate((0, 4)):
        value = product(part, 0, 1, begin, begin + 2)[0]
        spec_ref[0, :, 2 * NA * part : 2 * NA * part + NA] = value[:, :NA]
        spec_ref[0, :, 2 * NA * part + NA : 2 * NA * (part + 1)] = -value[:, NA:]
    of_re = product(0, 1, PAIRS, 0, 4)
    of_im = product(1, 1, PAIRS, 0, 4)
    c, s, cc, ss = (slice(NA * i, NA * (i + 1)) for i in range(4))
    spec_ref[1:, :, c] = of_re[..., c] + of_im[..., s]
    spec_ref[1:, :, s] = of_im[..., c] - of_re[..., s]
    spec_ref[1:, :, cc] = of_re[..., cc] - of_im[..., ss]
    spec_ref[1:, :, ss] = -(of_im[..., cc] + of_re[..., ss])
    total = jnp.zeros((count, NA), F32)
    for p in range(PAIRS):
        for part in range(2):
            re = spec_ref[p, :, 2 * NA * part : 2 * NA * part + NA]
            im = spec_ref[p, :, 2 * NA * part + NA : 2 * NA * part + 2 * NA]
            total += jnp.sqrt(re * re + im * im)
    high, low = split(total)
    low2 = (total - high.astype(F32) - low.astype(F32)).astype(BF16)
    row = lax.broadcasted_iota(jnp.int32, (NA, NA), 0)
    lane = lax.broadcasted_iota(jnp.int32, (NA, NA), 1)
    per_band = BAND // PH
    band = jnp.where(row // per_band == lane // per_band, 1.0, 0.0).astype(BF16)
    amplitude = (
        jnp.dot(
            jnp.concatenate([high, low, low2], axis=1),
            jnp.concatenate([band] * 3, axis=0),
            preferred_element_type=F32,
        )
        * (1.0 / BAND)
        + EPSILON
    )
    gain = 1.0 / amplitude
    gain = jnp.concatenate([gain] * 4, axis=1)
    for group in range(groups):
        at = slice(group * rows, group * rows + share)
        own = slice(group * rows + share, (group + 1) * rows)
        for p in range(PAIRS):
            src_ref[p, group] = (spec_ref[p, at] * gain[at]).astype(BF16)
            own_ref[p, group] = (spec_ref[p, own] * gain[own]).astype(BF16).astype(F32) * scale
    copies[1].wait()


def gather_lags(ends, re, im):
    half = PH // 2
    quarter = half // 2
    both = [None] + [re[p] + re[half - p] for p in range(1, quarter)]
    apart = [None] + [re[p] - re[half - p] for p in range(1, quarter)]
    oboth = [None] + [im[p] + im[half - p] for p in range(1, quarter)]
    oapart = [None] + [im[p] - im[half - p] for p in range(1, quarter)]
    edge = (ends[0] + ends[1], ends[0] - ends[1])
    cosines, sines = {}, {}
    for n in range(NN // 2 + 1):
        fold, total = (both, edge[0]) if n % 2 == 0 else (apart, edge[1])
        if n % 2 == 0:
            total = total + re[quarter] if (n // 2) % 2 == 0 else total - re[quarter]
        for p in range(1, quarter):
            c = math.cos(2 * math.pi * p * n / PH)
            if abs(abs(c) - 1) < 1e-9:
                total = total + fold[p] if c > 0 else total - fold[p]
            elif abs(c) > 1e-9:
                total = total + fold[p] * c
        cosines[n] = total
        if n:
            ofold = oapart if n % 2 == 0 else oboth
            total = None
            for p in range(1, quarter):
                s = math.sin(2 * math.pi * p * n / PH)
                if abs(s) > 1e-9:
                    term = ofold[p] if abs(s - 1) < 1e-9 else -ofold[p] if abs(s + 1) < 1e-9 else ofold[p] * s
                    total = term if total is None else total + term
            if n % 2:
                total = total + im[quarter] if n % 4 == 1 else total - im[quarter]
            sines[n] = total
    lags = []
    for n in range(-NN // 2, NN // 2):
        if n == 0:
            lags.append(cosines[0])
        else:
            lags.append(cosines[-n] + sines[-n] if n < 0 else cosines[n] - sines[n])
    return lags


def pair_kernel(last, group_size, own_ref, src_ref, table_ref, turn_ref, *refs):
    if last:
        done_ref, out_hbm, wide_ref, pair_a, pair_b, lag_a, lag_b, out_ref, sems = refs
    else:
        out_ref, wide_ref, pair_a, pair_b, lag_a, lag_b = refs
    groups, chans = own_ref.shape[1:3]
    share = src_ref.shape[2]
    size = group_size * chans
    copies = []

    def write(source, place, count):
        if last:
            copies.append(
                pltpu.make_async_copy(source, out_hbm.at[pl.ds(place, count)], sems.at[len(copies)])
            )
            copies[-1].start()

    if last:
        core = lax.axis_index("file") % 2
        write(done_ref, core * share, share)
        place = (1 - core) * share
    wide_ref[...] = src_ref[...].astype(F32)

    def finished(first):
        if last:
            write(out_ref.at[pl.ds(first, group_size)], place + first, group_size)

    def cross(first, pair_ref):
        for p in range(PAIRS):
            for part in range(2):
                left = 2 * NA * part
                own = [
                    (own_ref[p, g, :, left : left + NA], own_ref[p, g, :, left + NA : left + 2 * NA])
                    for g in range(groups)
                ]
                for s in range(0, group_size, 2):
                    res, ims = [], []
                    for one in range(2):
                        cre, cim = None, None
                        for g in range(groups):
                            at = first + s + one
                            sre = wide_ref[p, g, at : at + 1, left : left + NA]
                            sim = wide_ref[p, g, at : at + 1, left + NA : left + 2 * NA]
                            ore, oim = own[g]
                            tre = ore * sre + oim * sim
                            tim = oim * sre - ore * sim
                            cre = tre if cre is None else cre + tre
                            cim = tim if cim is None else cim + tim
                        res.append(cre)
                        ims.append(cim)
                    at = slice(s * chans, (s + 2) * chans)
                    pair_ref[p, at, left : left + NA] = jnp.concatenate(res, 0).astype(BF16)
                    pair_ref[p, at, left + NA : left + 2 * NA] = jnp.concatenate(ims, 0).astype(BF16)

    def product(pair_ref, lag_ref):
        lag_ref[0] = jnp.dot(pair_ref[0], table_ref[: 4 * NA], preferred_element_type=F32)
        lag_ref[1:] = jnp.dot(
            pair_ref[1:].reshape((PAIRS - 1) * size, 4 * NA),
            table_ref[4 * NA :],
            preferred_element_type=F32,
        ).reshape(PAIRS - 1, size, 2 * LO)

    def lags(first, lag_ref):
        for s in range(group_size):
            at = slice(s * chans, (s + 1) * chans)
            for h in range(HALF):
                lo = 128 * h
                ends = [lag_ref[0, at, LO * i + lo : LO * i + lo + 128] for i in range(2)]
                re, im = [None], [None]
                for p in range(1, PAIRS):
                    u = lag_ref[p, at, lo : lo + 128]
                    v = lag_ref[p, at, LO + lo : LO + lo + 128]
                    c = turn_ref[0, p, :, lo : lo + 128]
                    d = turn_ref[1, p, :, lo : lo + 128]
                    re.append(c * u - d * v)
                    im.append(c * v + d * u)
                for n, value in enumerate(gather_lags(ends, re, im)):
                    out_ref[first + s, :, LO * n + lo : LO * n + lo + 128] = value

    steps = share // group_size
    pairs, lagged = (pair_a, pair_b), (lag_a, lag_b)
    cross(0, pair_a)
    for i in range(steps):
        product(pairs[i % 2], lagged[i % 2])
        if i + 1 < steps:
            cross((i + 1) * group_size, pairs[(i + 1) % 2])
        if i:
            lags((i - 1) * group_size, lagged[(i - 1) % 2])
            finished((i - 1) * group_size)
    lags((steps - 1) * group_size, lagged[(steps - 1) % 2])
    finished((steps - 1) * group_size)
    for copy in copies:
        copy.wait()


def pair_call(own, src, table, turn, done=None):
    groups, chans = own.shape[1:3]
    share = src.shape[2]
    vmem = pl.BlockSpec(memory_space=pltpu.VMEM)
    hbm = pl.BlockSpec(memory_space=pltpu.HBM)
    last = done is not None
    group_size = min(GROUPS[last], share)
    operands = [own, src, table, turn] + [done] * last
    scratch = [pltpu.VMEM((PAIRS, groups, share, 4 * NA), F32)]
    scratch += [pltpu.VMEM((PAIRS, group_size * chans, 4 * NA), BF16)] * 2
    scratch += [pltpu.VMEM((PAIRS, group_size * chans, 2 * LO), F32)] * 2
    if last:
        scratch += [
            pltpu.VMEM((share, chans, SEG), F32),
            pltpu.SemaphoreType.DMA((1 + share // group_size,)),
        ]
    return pl.pallas_call(
        functools.partial(pair_kernel, last, group_size),
        in_specs=[vmem] * len(operands),
        out_specs=hbm if last else vmem,
        scratch_shapes=scratch,
        out_shape=jax.ShapeDtypeStruct((share * (2 if last else 1), chans, SEG), F32),
        compiler_params=pltpu.CompilerParams(vmem_limit_bytes=32 * 2**20),
        name="pair_last" if last else "pair_first",
    )(*operands)


def local(raw, fir_taps, offsets, vs_index):
    samples = raw[0]
    channels = samples.shape[0]
    files = lax.axis_size("file")
    wins = lax.axis_size("win")
    sources = vs_index.shape[0] // wins
    share = sources // 2
    chans = channels // files
    rows = share + chans
    segs = files * TD // SEG
    groups = wins * segs
    taps = fir_taps[None, :]
    index = vs_index[None, :]
    table = transform_table()
    scale = 1.0 / math.sqrt(SEG * segs * wins)
    hbm = pl.BlockSpec(memory_space=pltpu.HBM)
    vmem = pl.BlockSpec(memory_space=pltpu.VMEM)
    packed = pl.pallas_call(
        functools.partial(decimate_kernel, files, wins),
        out_shape=jax.ShapeDtypeStruct((files * wins, 2 * chans + rows, TD), BF16),
        in_specs=[hbm] * 4,
        out_specs=vmem,
        scratch_shapes=[
            pltpu.SMEM(offsets.shape, jnp.int32),
            pltpu.VMEM(taps.shape, F32),
            pltpu.VMEM(index.shape, jnp.int32),
            pltpu.VMEM(samples.shape, BF16),
            pltpu.SemaphoreType.DMA((4,)),
        ],
        compiler_params=pltpu.CompilerParams(vmem_limit_bytes=60 * 2**20),
        name="decimate",
    )(offsets, taps, index, samples)
    data = lax.all_to_all(packed, ("file", "win"), split_axis=0, concat_axis=0, tiled=True)
    own, src, table_high, turn = pl.pallas_call(
        functools.partial(forward_kernel, files, wins, chans, scale),
        out_shape=(
            jax.ShapeDtypeStruct((PAIRS, groups, chans, 4 * NA), F32),
            jax.ShapeDtypeStruct((PAIRS, groups, share, 4 * NA), BF16),
            jax.ShapeDtypeStruct((8 * NA, 2 * LO), BF16),
            jax.ShapeDtypeStruct((2, PAIRS, 8, LO), F32),
        ),
        in_specs=[vmem, hbm],
        out_specs=(vmem, vmem, vmem, vmem),
        scratch_shapes=[
            pltpu.VMEM((6 * NA, 2 * LO), BF16),
            pltpu.VMEM((files * wins, rows, TD), F32),
            pltpu.VMEM((2, PAIRS, groups * rows, LO), BF16),
            pltpu.VMEM((2, PAIRS, groups * rows, LO), BF16),
            pltpu.VMEM((PAIRS, groups * rows, 4 * NA), F32),
            pltpu.SemaphoreType.DMA((2,)),
        ],
        compiler_params=pltpu.CompilerParams(vmem_limit_bytes=103 * 2**19),
        name="forward",
    )(data, table)
    other = lax.ppermute(src, "file", [(i, i ^ 1) for i in range(files)])
    half = pair_call(own, src, table_high, turn)
    return pair_call(own, other, table_high, turn, half)


def solution(mesh):
    return jax.shard_map(
        local,
        mesh=mesh,
        in_specs=(P("win", None, "file"), P(), P("win", "file"), P()),
        out_specs=P("win", "file", None),
        check_vma=False,
    )
```

```python
import functools
import math

import jax
import jax.numpy as jnp
import numpy as np
from jax import lax
from jax.experimental import pallas as pl
from jax.experimental.pallas import tpu as pltpu
from jax.sharding import PartitionSpec as P

R = 10
TAPS = 64
TD = 128
SEG = 2048
BAND = 64
EPSILON = 1e-06

PH = 16
LO = 256
NA = SEG // PH
NN = SEG // LO
HALF = LO // 128
PAIRS = PH // 2
EARLY = 8
GROUPS = (8, 8)
TABLE_ROWS = 2048

NT = (((1,), (1,)), ((), ()))
NN_DIMS = (((1,), (0,)), ((), ()))
F32 = jnp.float32
BF16 = jnp.bfloat16


def transform_table():
    a = np.arange(NA)[:, None]
    m = np.arange(LO)[None, :]

    def wave(f):
        angle = 2 * np.pi * ((f * m) % (2 * SEG)) / (2 * SEG)
        return np.cos(angle), np.sin(angle)

    c, s = wave(PH * a)
    cc, ss = wave(PH * (a + 1))
    folded = np.block([[c, s], [-s, c], [cc, -ss], [-ss, -cc]])
    c8, s8 = wave(PH * a + PH // 2)
    z = np.zeros_like(c)
    ends = np.block([[c, z], [-s, z], [z, c8], [z, -s8]])
    waves = np.concatenate([c, s, cc, ss, c8, s8])
    high = waves.astype(BF16)
    low = (waves - high.astype(np.float64)).astype(BF16)
    inverse = np.concatenate([ends, folded]).astype(BF16)
    parts = [inverse, np.concatenate([high, low], axis=1)]
    spare = TABLE_ROWS - sum(len(part) for part in parts)
    return jnp.asarray(np.concatenate(parts + [np.zeros((spare, 2 * LO), BF16)]))


def three_pass(high, low, table_high, table_low, dims):
    dot = functools.partial(lax.dot_general, dimension_numbers=dims, preferred_element_type=F32)
    return dot(high, table_high) + (dot(low, table_high) + dot(high, table_low))


def split(x):
    high = x.astype(BF16)
    return high, (x - high.astype(F32)).astype(BF16)


def decimate_kernel(
    files, wins,
    offset_hbm, taps_hbm, index_hbm, raw_hbm, out_ref,
    offset_ref, taps_ref, index_ref, raw_ref, sems,
):
    copies = [
        pltpu.make_async_copy(source, target, sems.at[i])
        for i, (source, target) in enumerate(
            (
                (offset_hbm, offset_ref),
                (taps_hbm, taps_ref),
                (index_hbm, index_ref),
                (raw_hbm, raw_ref),
            )
        )
    ]
    for copy in copies:
        copy.start()
    channels, samples = raw_ref.shape
    half = TD // 2
    stride = R * half
    width = stride + 128
    copies[0].wait()
    copies[1].wait()
    offset = offset_ref[0, 0]
    taps = jnp.broadcast_to(taps_ref[...], (half, TAPS)).astype(BF16)
    k = lax.broadcasted_iota(jnp.int32, (TAPS, 256), 0)
    lane = lax.broadcasted_iota(jnp.int32, (TAPS, 256), 1)
    place = jnp.where(lane == 128 - k, 1.0, 0.0).astype(BF16)
    band = jnp.dot(taps, place, preferred_element_type=F32)
    band = pltpu.roll(band[:8], offset, 1)
    row = lax.broadcasted_iota(jnp.int32, (8, 256), 0)
    for bit in range(3):
        band = jnp.where((row >> bit) % 2 == 1, pltpu.roll(band, R << bit, 1), band)
    band = jnp.concatenate([band, jnp.zeros((8, width - 256), F32)], axis=1)
    tiles = [band if not i else pltpu.roll(band, 8 * R * i, 1) for i in range(half // 8)]
    rolled = jnp.concatenate(tiles, axis=0).astype(BF16)
    zero = jnp.zeros((half, width), BF16)
    first = jnp.concatenate([rolled, zero], axis=0)
    second = jnp.concatenate([zero, rolled], axis=0)
    copies[2].wait()
    sources = index_ref.shape[1]
    row = lax.broadcasted_iota(jnp.int32, (channels, sources), 0)
    pick = jnp.where(row == index_ref[...], 1.0, 0.0).astype(BF16)
    copies[3].wait()
    total = lax.dot_general(
        raw_ref[:, stride - 128 : 2 * stride], second, NT, preferred_element_type=F32
    )
    total += lax.dot_general(raw_ref[:, :stride], first[:, 128:], NT, preferred_element_type=F32)
    decimated = total.astype(BF16)
    lane = lax.broadcasted_iota(jnp.int32, (channels, 128), 1)
    low = jnp.where(lane < EARLY, total - decimated.astype(F32), 0.0)
    tail = raw_ref[:, samples - 128 :].astype(F32)
    tail = jnp.where(lane == TAPS, offset.astype(F32), tail)
    everything = jnp.concatenate([decimated, tail.astype(BF16), low.astype(BF16)], axis=1)
    chosen = lax.dot_general(
        pick, everything, (((0,), (0,)), ((), ())), preferred_element_type=F32
    )
    per_win = sources // wins
    share = per_win // 2
    per_file = channels // files
    lower = lane[:per_file] < 64

    def low_lanes(value, i):
        return pltpu.roll(value, 64 + EARLY * i, 1)

    wide = jnp.concatenate([taps_ref[...], jnp.zeros((1, 128 - TAPS), F32)], axis=1)
    row = lax.broadcasted_iota(jnp.int32, (per_file, 128), 0)
    carried = jnp.where(row == 0, pltpu.roll(wide, 96, 1), pltpu.roll(wide, 64, 1))
    carried = jnp.where((row < 2) & (lane[:per_file] >= 96), carried, 0.0)
    blocks = {}
    for win in range(wins):
        for core in range(2):
            at = win * per_win + core * share
            part = chosen[at : at + share]
            tails = pltpu.roll(part[:, 128:256], 64, 1)
            lows = part[:, 256:]
            packed = carried + low_lanes(lows[:per_file], 0)
            for i in range(1, share // per_file):
                packed += low_lanes(lows[i * per_file : (i + 1) * per_file], i)
            second = tails[per_file:] if share > per_file else jnp.zeros_like(packed)
            blocks[win, core] = (
                part[:, :128].astype(BF16), tails[:per_file], jnp.where(lower, second, packed)
            )
    for file in range(files):
        own = slice(file * per_file, (file + 1) * per_file)
        own_low = low_lanes(low[own], share // per_file)
        for win in range(wins):
            dest = file * wins + win
            dec, tails, packed = blocks[win, file % 2]
            out_ref[dest, : 2 * per_file, :] = jnp.concatenate(
                [jnp.where(lower, tails, tail[own]), packed + own_low], axis=0
            ).astype(BF16)
            out_ref[dest, 2 * per_file : 2 * per_file + share, :] = dec
            out_ref[dest, 2 * per_file + share :, :] = decimated[own]


def spread(x):
    terms = []
    for p in range(PH // 2 + 1):
        re, im = None, None
        for n in range(NN):
            angle = (p * n) % PH
            c, s = math.cos(2 * math.pi * angle / PH), -math.sin(2 * math.pi * angle / PH)
            if angle % (PH // 4):
                re = x[n] * c if re is None else re + x[n] * c
                im = x[n] * s if im is None else im + x[n] * s
            elif angle % (PH // 2):
                im = x[n] * round(s) if im is None else (im + x[n] if s > 0 else im - x[n])
            else:
                re = x[n] if re is None else (re + x[n] if c > 0 else re - x[n])
        terms.append((re, im))
    return terms


def forward_kernel(
    files, wins, chans, scale,
    data_ref, table_hbm, own_ref, src_ref, table_ref, turn_ref,
    waves_ref, fixed_ref, high_ref, low_ref, spec_ref, sems,
):
    copies = [
        pltpu.make_async_copy(source, target, sems.at[i])
        for i, (source, target) in enumerate(
            (
                (table_hbm.at[pl.ds(8 * NA, 6 * NA)], waves_ref),
                (table_hbm.at[pl.ds(0, 8 * NA)], table_ref),
            )
        )
    ]
    copies[0].start()
    phase = lax.broadcasted_iota(jnp.int32, (8, LO), 0) * lax.broadcasted_iota(jnp.int32, (8, LO), 1)
    angle = phase.astype(F32) * (math.pi / SEG)
    turns = (jnp.cos(angle), jnp.sin(angle))
    for p in range(PAIRS):
        for i in range(2):
            turn_ref[i, p] = jnp.broadcast_to(turns[i][p : p + 1], (8, LO))
    rows = fixed_ref.shape[1]
    share = rows - chans
    lead = 2 * chans
    segs = files * TD // SEG
    per_seg = files // segs
    devices = files * wins

    first = data_ref[0, chans : 2 * chans, :].astype(F32)
    row = lax.broadcasted_iota(jnp.int32, (TAPS, 128), 0)
    lane = lax.broadcasted_iota(jnp.int32, (TAPS, 128), 1)
    taps = jnp.where(lane[:1] < 32, pltpu.roll(first[:1], 32, 1), pltpu.roll(first[1:2], 64, 1))
    share_of = jnp.where(lane < TAPS, jnp.broadcast_to(taps, (TAPS, 128)), 0.0)
    for bit in range(6):
        move = (TAPS - row) >> bit
        share_of = jnp.where(move % 2 == 1, pltpu.roll(share_of, 128 - (1 << bit), 1), share_of)
    share_of = jnp.where((lane < row) & (row > 0), share_of, 0.0).astype(BF16)
    nothing = jnp.zeros((TAPS, 128), BF16)
    row = lax.broadcasted_iota(jnp.int32, (128, 128), 0)
    lane = lax.broadcasted_iota(jnp.int32, (128, 128), 1)
    columns = [
        jnp.concatenate([share_of, nothing], axis=0),
        jnp.concatenate([nothing, share_of], axis=0),
        jnp.where(row == 0, 1.0, 0.0).astype(BF16),
    ]
    for i in range(rows // chans):
        columns.append(
            jnp.where((row == 64 + EARLY * i + lane) & (lane < EARLY), 1.0, 0.0).astype(BF16)
        )
    collapse = jnp.where((row // R == lane) & (lane < EARLY), 1.0, 0.0).astype(BF16)
    tails = data_ref[:, :lead, :].reshape(devices * lead, 128)
    mixed = jnp.dot(tails, jnp.concatenate(columns, axis=1), preferred_element_type=F32)
    mixed = mixed.reshape(devices, lead, len(columns) * 128)
    residue = (lax.broadcasted_iota(jnp.int32, (1, 1, 128), 2) % R).astype(F32)
    offset = mixed[wins:, :, 256:384]

    def early(value, kept):
        value = jnp.where(residue == offset[:, :kept], value[:-wins, :kept], 0.0)
        value = value.reshape((devices - wins) * kept, 128)
        high, low = split(value)
        value = jnp.dot(high, collapse, preferred_element_type=F32) + jnp.dot(
            low, collapse, preferred_element_type=F32
        )
        value = value.reshape(devices - wins, kept, 128)
        return jnp.concatenate([jnp.zeros((wins, kept, 128), F32), value], axis=0)

    added = jnp.concatenate(
        [early(mixed[:, :, :128], share), early(mixed[:, :, 128:256], chans)], axis=1
    )
    lows = jnp.concatenate(
        [
            mixed[:, chans:, 128 * (3 + i) : 128 * (4 + i)]
            for i in range(rows // chans)
        ],
        axis=1,
    )
    fixed_ref[...] = (data_ref[:, lead:, :].astype(F32) + (lows + added)).astype(BF16).astype(F32)

    for win in range(wins):
        for seg in range(segs):
            base = (win * segs + seg) * rows
            for h in range(HALF):
                x = [fixed_ref[(seg * per_seg + HALF * n + h) * wins + win] for n in range(NN)]
                terms = spread(x)
                for p in range(PAIRS):
                    if p:
                        re, im = terms[p]
                        c = turn_ref[0, p, :1, 128 * h : 128 * h + 128]
                        s = turn_ref[1, p, :1, 128 * h : 128 * h + 128]
                        re, im = re * c + im * s, im * c - re * s
                    else:
                        re, im = terms[0][0], terms[PAIRS][0]
                    for part, value in enumerate((re, im)):
                        at = slice(128 * h, 128 * h + 128)
                        high, low = split(value)
                        high_ref[part, p, base : base + rows, at] = high
                        low_ref[part, p, base : base + rows, at] = low
    groups = wins * segs
    count = groups * rows
    copies[0].wait()
    copies[1].start()

    def product(part, first, last, begin, end):
        lines = (last - first) * count
        return three_pass(
            high_ref[part, first:last].reshape(lines, LO),
            low_ref[part, first:last].reshape(lines, LO),
            waves_ref[begin * NA : end * NA, :LO],
            waves_ref[begin * NA : end * NA, LO:],
            NT,
        ).reshape(last - first, count, (end - begin) * NA)

    for part, begin in enumerate((0, 4)):
        value = product(part, 0, 1, begin, begin + 2)[0]
        spec_ref[0, :, 2 * NA * part : 2 * NA * part + NA] = value[:, :NA]
        spec_ref[0, :, 2 * NA * part + NA : 2 * NA * (part + 1)] = -value[:, NA:]
    of_re = product(0, 1, PAIRS, 0, 4)
    of_im = product(1, 1, PAIRS, 0, 4)
    c, s, cc, ss = (slice(NA * i, NA * (i + 1)) for i in range(4))
    spec_ref[1:, :, c] = of_re[..., c] + of_im[..., s]
    spec_ref[1:, :, s] = of_im[..., c] - of_re[..., s]
    spec_ref[1:, :, cc] = of_re[..., cc] - of_im[..., ss]
    spec_ref[1:, :, ss] = -(of_im[..., cc] + of_re[..., ss])
    total = jnp.zeros((count, NA), F32)
    for p in range(PAIRS):
        for part in range(2):
            re = spec_ref[p, :, 2 * NA * part : 2 * NA * part + NA]
            im = spec_ref[p, :, 2 * NA * part + NA : 2 * NA * part + 2 * NA]
            total += jnp.sqrt(re * re + im * im)
    high, low = split(total)
    low2 = (total - high.astype(F32) - low.astype(F32)).astype(BF16)
    row = lax.broadcasted_iota(jnp.int32, (NA, NA), 0)
    lane = lax.broadcasted_iota(jnp.int32, (NA, NA), 1)
    per_band = BAND // PH
    band = jnp.where(row // per_band == lane // per_band, 1.0, 0.0).astype(BF16)
    amplitude = (
        jnp.dot(
            jnp.concatenate([high, low, low2], axis=1),
            jnp.concatenate([band] * 3, axis=0),
            preferred_element_type=F32,
        )
        * (1.0 / BAND)
        + EPSILON
    )
    gain = 1.0 / amplitude
    gain = jnp.concatenate([gain] * 4, axis=1)
    for group in range(groups):
        at = slice(group * rows, group * rows + share)
        own = slice(group * rows + share, (group + 1) * rows)
        for p in range(PAIRS):
            src_ref[p, group] = (spec_ref[p, at] * gain[at]).astype(BF16)
            own_ref[p, group] = (spec_ref[p, own] * gain[own]).astype(BF16).astype(F32) * scale
    copies[1].wait()


def gather_lags(ends, re, im):
    half = PH // 2
    quarter = half // 2
    both = [None] + [re[p] + re[half - p] for p in range(1, quarter)]
    apart = [None] + [re[p] - re[half - p] for p in range(1, quarter)]
    oboth = [None] + [im[p] + im[half - p] for p in range(1, quarter)]
    oapart = [None] + [im[p] - im[half - p] for p in range(1, quarter)]
    edge = (ends[0] + ends[1], ends[0] - ends[1])
    cosines, sines = {}, {}
    for n in range(NN // 2 + 1):
        fold, total = (both, edge[0]) if n % 2 == 0 else (apart, edge[1])
        if n % 2 == 0:
            total = total + re[quarter] if (n // 2) % 2 == 0 else total - re[quarter]
        for p in range(1, quarter):
            c = math.cos(2 * math.pi * p * n / PH)
            if abs(abs(c) - 1) < 1e-9:
                total = total + fold[p] if c > 0 else total - fold[p]
            elif abs(c) > 1e-9:
                total = total + fold[p] * c
        cosines[n] = total
        if n:
            ofold = oapart if n % 2 == 0 else oboth
            total = None
            for p in range(1, quarter):
                s = math.sin(2 * math.pi * p * n / PH)
                if abs(s) > 1e-9:
                    term = ofold[p] if abs(s - 1) < 1e-9 else -ofold[p] if abs(s + 1) < 1e-9 else ofold[p] * s
                    total = term if total is None else total + term
            if n % 2:
                total = total + im[quarter] if n % 4 == 1 else total - im[quarter]
            sines[n] = total
    lags = []
    for n in range(-NN // 2, NN // 2):
        if n == 0:
            lags.append(cosines[0])
        else:
            lags.append(cosines[-n] + sines[-n] if n < 0 else cosines[n] - sines[n])
    return lags


def pair_kernel(last, group_size, own_ref, src_ref, table_ref, turn_ref, *refs):
    if last:
        done_ref, out_hbm, wide_ref, pair_a, pair_b, lag_a, lag_b, out_ref, sems = refs
    else:
        out_ref, wide_ref, pair_a, pair_b, lag_a, lag_b = refs
    groups, chans = own_ref.shape[1:3]
    share = src_ref.shape[2]
    size = group_size * chans
    copies = []

    def write(source, place, count):
        if last:
            copies.append(
                pltpu.make_async_copy(source, out_hbm.at[pl.ds(place, count)], sems.at[len(copies)])
            )
            copies[-1].start()

    if last:
        core = lax.axis_index("file") % 2
        write(done_ref, core * share, share)
        place = (1 - core) * share
    wide_ref[...] = src_ref[...].astype(F32)

    def cross(first, pair_ref):
        for p in range(PAIRS):
            for part in range(2):
                left = 2 * NA * part
                own = [
                    (own_ref[p, g, :, left : left + NA], own_ref[p, g, :, left + NA : left + 2 * NA])
                    for g in range(groups)
                ]
                for s in range(0, group_size, 2):
                    res, ims = [], []
                    for one in range(2):
                        cre, cim = None, None
                        for g in range(groups):
                            at = first + s + one
                            sre = wide_ref[p, g, at : at + 1, left : left + NA]
                            sim = wide_ref[p, g, at : at + 1, left + NA : left + 2 * NA]
                            ore, oim = own[g]
                            tre = ore * sre + oim * sim
                            tim = oim * sre - ore * sim
                            cre = tre if cre is None else cre + tre
                            cim = tim if cim is None else cim + tim
                        res.append(cre)
                        ims.append(cim)
                    at = slice(s * chans, (s + 2) * chans)
                    pair_ref[p, at, left : left + NA] = jnp.concatenate(res, 0).astype(BF16)
                    pair_ref[p, at, left + NA : left + 2 * NA] = jnp.concatenate(ims, 0).astype(BF16)

    def product(pair_ref, lag_ref):
        lag_ref[0] = jnp.dot(pair_ref[0], table_ref[: 4 * NA], preferred_element_type=F32)
        lag_ref[1:] = jnp.dot(
            pair_ref[1:].reshape((PAIRS - 1) * size, 4 * NA),
            table_ref[4 * NA :],
            preferred_element_type=F32,
        ).reshape(PAIRS - 1, size, 2 * LO)

    def lags(first, lag_ref):
        for s in range(group_size):
            at = slice(s * chans, (s + 1) * chans)
            for h in range(HALF):
                lo = 128 * h
                ends = [lag_ref[0, at, LO * i + lo : LO * i + lo + 128] for i in range(2)]
                re, im = [None], [None]
                for p in range(1, PAIRS):
                    u = lag_ref[p, at, lo : lo + 128]
                    v = lag_ref[p, at, LO + lo : LO + lo + 128]
                    c = turn_ref[0, p, :, lo : lo + 128]
                    d = turn_ref[1, p, :, lo : lo + 128]
                    re.append(c * u - d * v)
                    im.append(c * v + d * u)
                for n, value in enumerate(gather_lags(ends, re, im)):
                    out_ref[first + s, :, LO * n + lo : LO * n + lo + 128] = value
            if last:
                write(out_ref.at[pl.ds(first + s, 1)], place + first + s, 1)

    steps = share // group_size
    pairs, lagged = (pair_a, pair_b), (lag_a, lag_b)
    cross(0, pair_a)
    for i in range(steps):
        product(pairs[i % 2], lagged[i % 2])
        if i + 1 < steps:
            cross((i + 1) * group_size, pairs[(i + 1) % 2])
        if i:
            lags((i - 1) * group_size, lagged[(i - 1) % 2])
    lags((steps - 1) * group_size, lagged[(steps - 1) % 2])
    for copy in copies:
        copy.wait()


def pair_call(own, src, table, turn, done=None):
    groups, chans = own.shape[1:3]
    share = src.shape[2]
    vmem = pl.BlockSpec(memory_space=pltpu.VMEM)
    hbm = pl.BlockSpec(memory_space=pltpu.HBM)
    last = done is not None
    group_size = min(GROUPS[last], share)
    operands = [own, src, table, turn] + [done] * last
    scratch = [pltpu.VMEM((PAIRS, groups, share, 4 * NA), F32)]
    scratch += [pltpu.VMEM((PAIRS, group_size * chans, 4 * NA), BF16)] * 2
    scratch += [pltpu.VMEM((PAIRS, group_size * chans, 2 * LO), F32)] * 2
    if last:
        scratch += [
            pltpu.VMEM((share, chans, SEG), F32),
            pltpu.SemaphoreType.DMA((1 + share,)),
        ]
    return pl.pallas_call(
        functools.partial(pair_kernel, last, group_size),
        in_specs=[vmem] * len(operands),
        out_specs=hbm if last else vmem,
        scratch_shapes=scratch,
        out_shape=jax.ShapeDtypeStruct((share * (2 if last else 1), chans, SEG), F32),
        compiler_params=pltpu.CompilerParams(vmem_limit_bytes=32 * 2**20),
        name="pair_last" if last else "pair_first",
    )(*operands)


def local(raw, fir_taps, offsets, vs_index):
    samples = raw[0]
    channels = samples.shape[0]
    files = lax.axis_size("file")
    wins = lax.axis_size("win")
    sources = vs_index.shape[0] // wins
    share = sources // 2
    chans = channels // files
    rows = share + chans
    segs = files * TD // SEG
    groups = wins * segs
    taps = fir_taps[None, :]
    index = vs_index[None, :]
    table = transform_table()
    scale = 1.0 / math.sqrt(SEG * segs * wins)
    hbm = pl.BlockSpec(memory_space=pltpu.HBM)
    vmem = pl.BlockSpec(memory_space=pltpu.VMEM)
    packed = pl.pallas_call(
        functools.partial(decimate_kernel, files, wins),
        out_shape=jax.ShapeDtypeStruct((files * wins, 2 * chans + rows, TD), BF16),
        in_specs=[hbm] * 4,
        out_specs=vmem,
        scratch_shapes=[
            pltpu.SMEM(offsets.shape, jnp.int32),
            pltpu.VMEM(taps.shape, F32),
            pltpu.VMEM(index.shape, jnp.int32),
            pltpu.VMEM(samples.shape, BF16),
            pltpu.SemaphoreType.DMA((4,)),
        ],
        compiler_params=pltpu.CompilerParams(vmem_limit_bytes=60 * 2**20),
        name="decimate",
    )(offsets, taps, index, samples)
    data = lax.all_to_all(packed, ("file", "win"), split_axis=0, concat_axis=0, tiled=True)
    own, src, table_high, turn = pl.pallas_call(
        functools.partial(forward_kernel, files, wins, chans, scale),
        out_shape=(
            jax.ShapeDtypeStruct((PAIRS, groups, chans, 4 * NA), F32),
            jax.ShapeDtypeStruct((PAIRS, groups, share, 4 * NA), BF16),
            jax.ShapeDtypeStruct((8 * NA, 2 * LO), BF16),
            jax.ShapeDtypeStruct((2, PAIRS, 8, LO), F32),
        ),
        in_specs=[vmem, hbm],
        out_specs=(vmem, vmem, vmem, vmem),
        scratch_shapes=[
            pltpu.VMEM((6 * NA, 2 * LO), BF16),
            pltpu.VMEM((files * wins, rows, TD), F32),
            pltpu.VMEM((2, PAIRS, groups * rows, LO), BF16),
            pltpu.VMEM((2, PAIRS, groups * rows, LO), BF16),
            pltpu.VMEM((PAIRS, groups * rows, 4 * NA), F32),
            pltpu.SemaphoreType.DMA((2,)),
        ],
        compiler_params=pltpu.CompilerParams(vmem_limit_bytes=103 * 2**19),
        name="forward",
    )(data, table)
    other = lax.ppermute(src, "file", [(i, i ^ 1) for i in range(files)])
    half = pair_call(own, src, table_high, turn)
    return pair_call(own, other, table_high, turn, half)


def solution(mesh):
    return jax.shard_map(
        local,
        mesh=mesh,
        in_specs=(P("win", None, "file"), P(), P("win", "file"), P()),
        out_specs=P("win", "file", None),
        check_vma=False,
    )
```

```python
import functools
import math

import jax
import jax.numpy as jnp
import numpy as np
from jax import lax
from jax.experimental import pallas as pl
from jax.experimental.pallas import tpu as pltpu
from jax.sharding import PartitionSpec as P

R = 10
TAPS = 64
TD = 128
SEG = 2048
BAND = 64
EPSILON = 1e-06

PH = 16
LO = 256
NA = SEG // PH
NN = SEG // LO
HALF = LO // 128
PAIRS = PH // 2
EARLY = 8
GROUPS = (16, 8)
TABLE_ROWS = 2048

NT = (((1,), (1,)), ((), ()))
NN_DIMS = (((1,), (0,)), ((), ()))
F32 = jnp.float32
BF16 = jnp.bfloat16


def transform_table():
    a = np.arange(NA)[:, None]
    m = np.arange(LO)[None, :]

    def wave(f):
        angle = 2 * np.pi * ((f * m) % (2 * SEG)) / (2 * SEG)
        return np.cos(angle), np.sin(angle)

    c, s = wave(PH * a)
    cc, ss = wave(PH * (a + 1))
    folded = np.block([[c, s], [-s, c], [cc, -ss], [-ss, -cc]])
    c8, s8 = wave(PH * a + PH // 2)
    z = np.zeros_like(c)
    ends = np.block([[c, z], [-s, z], [z, c8], [z, -s8]])
    waves = np.concatenate([c, s, cc, ss, c8, s8])
    high = waves.astype(BF16)
    low = (waves - high.astype(np.float64)).astype(BF16)
    inverse = np.concatenate([ends, folded]).astype(BF16)
    parts = [inverse, np.concatenate([high, low], axis=1)]
    spare = TABLE_ROWS - sum(len(part) for part in parts)
    return jnp.asarray(np.concatenate(parts + [np.zeros((spare, 2 * LO), BF16)]))


def three_pass(high, low, table_high, table_low, dims):
    dot = functools.partial(lax.dot_general, dimension_numbers=dims, preferred_element_type=F32)
    return dot(high, table_high) + (dot(low, table_high) + dot(high, table_low))


def split(x):
    high = x.astype(BF16)
    return high, (x - high.astype(F32)).astype(BF16)


def decimate_kernel(
    files, wins,
    offset_hbm, taps_hbm, index_hbm, raw_hbm, out_ref,
    offset_ref, taps_ref, index_ref, raw_ref, sems,
):
    copies = [
        pltpu.make_async_copy(source, target, sems.at[i])
        for i, (source, target) in enumerate(
            (
                (offset_hbm, offset_ref),
                (taps_hbm, taps_ref),
                (index_hbm, index_ref),
                (raw_hbm, raw_ref),
            )
        )
    ]
    for copy in copies:
        copy.start()
    channels, samples = raw_ref.shape
    half = TD // 2
    stride = R * half
    width = stride + 128
    copies[0].wait()
    copies[1].wait()
    offset = offset_ref[0, 0]
    taps = jnp.broadcast_to(taps_ref[...], (half, TAPS)).astype(BF16)
    k = lax.broadcasted_iota(jnp.int32, (TAPS, 256), 0)
    lane = lax.broadcasted_iota(jnp.int32, (TAPS, 256), 1)
    place = jnp.where(lane == 128 - k, 1.0, 0.0).astype(BF16)
    band = jnp.dot(taps, place, preferred_element_type=F32)
    band = pltpu.roll(band[:8], offset, 1)
    row = lax.broadcasted_iota(jnp.int32, (8, 256), 0)
    for bit in range(3):
        band = jnp.where((row >> bit) % 2 == 1, pltpu.roll(band, R << bit, 1), band)
    band = jnp.concatenate([band, jnp.zeros((8, width - 256), F32)], axis=1)
    tiles = [band if not i else pltpu.roll(band, 8 * R * i, 1) for i in range(half // 8)]
    rolled = jnp.concatenate(tiles, axis=0).astype(BF16)
    zero = jnp.zeros((half, width), BF16)
    first = jnp.concatenate([rolled, zero], axis=0)
    second = jnp.concatenate([zero, rolled], axis=0)
    copies[2].wait()
    sources = index_ref.shape[1]
    row = lax.broadcasted_iota(jnp.int32, (channels, sources), 0)
    pick = jnp.where(row == index_ref[...], 1.0, 0.0).astype(BF16)
    copies[3].wait()
    total = lax.dot_general(
        raw_ref[:, stride - 128 : 2 * stride], second, NT, preferred_element_type=F32
    )
    total += lax.dot_general(raw_ref[:, :stride], first[:, 128:], NT, preferred_element_type=F32)
    decimated = total.astype(BF16)
    lane = lax.broadcasted_iota(jnp.int32, (channels, 128), 1)
    low = jnp.where(lane < EARLY, total - decimated.astype(F32), 0.0)
    tail = raw_ref[:, samples - 128 :].astype(F32)
    tail = jnp.where(lane == TAPS, offset.astype(F32), tail)
    everything = jnp.concatenate([decimated, tail.astype(BF16), low.astype(BF16)], axis=1)
    chosen = lax.dot_general(
        pick, everything, (((0,), (0,)), ((), ())), preferred_element_type=F32
    )
    per_win = sources // wins
    share = per_win // 2
    per_file = channels // files
    lower = lane[:per_file] < 64

    def low_lanes(value, i):
        return pltpu.roll(value, 64 + EARLY * i, 1)

    wide = jnp.concatenate([taps_ref[...], jnp.zeros((1, 128 - TAPS), F32)], axis=1)
    row = lax.broadcasted_iota(jnp.int32, (per_file, 128), 0)
    carried = jnp.where(row == 0, pltpu.roll(wide, 96, 1), pltpu.roll(wide, 64, 1))
    carried = jnp.where((row < 2) & (lane[:per_file] >= 96), carried, 0.0)
    blocks = {}
    for win in range(wins):
        for core in range(2):
            at = win * per_win + core * share
            part = chosen[at : at + share]
            tails = pltpu.roll(part[:, 128:256], 64, 1)
            lows = part[:, 256:]
            packed = carried + low_lanes(lows[:per_file], 0)
            for i in range(1, share // per_file):
                packed += low_lanes(lows[i * per_file : (i + 1) * per_file], i)
            second = tails[per_file:] if share > per_file else jnp.zeros_like(packed)
            blocks[win, core] = (
                part[:, :128].astype(BF16), tails[:per_file], jnp.where(lower, second, packed)
            )
    for file in range(files):
        own = slice(file * per_file, (file + 1) * per_file)
        own_low = low_lanes(low[own], share // per_file)
        for win in range(wins):
            dest = file * wins + win
            dec, tails, packed = blocks[win, file % 2]
            out_ref[dest, : 2 * per_file, :] = jnp.concatenate(
                [jnp.where(lower, tails, tail[own]), packed + own_low], axis=0
            ).astype(BF16)
            out_ref[dest, 2 * per_file : 2 * per_file + share, :] = dec
            out_ref[dest, 2 * per_file + share :, :] = decimated[own]


def spread(x):
    terms = []
    for p in range(PH // 2 + 1):
        re, im = None, None
        for n in range(NN):
            angle = (p * n) % PH
            c, s = math.cos(2 * math.pi * angle / PH), -math.sin(2 * math.pi * angle / PH)
            if angle % (PH // 4):
                re = x[n] * c if re is None else re + x[n] * c
                im = x[n] * s if im is None else im + x[n] * s
            elif angle % (PH // 2):
                im = x[n] * round(s) if im is None else (im + x[n] if s > 0 else im - x[n])
            else:
                re = x[n] if re is None else (re + x[n] if c > 0 else re - x[n])
        terms.append((re, im))
    return terms


def forward_kernel(
    files, wins, chans, scale,
    data_ref, table_hbm, own_ref, src_ref, table_ref, turn_ref,
    waves_ref, fixed_ref, high_ref, low_ref, spec_ref, sems,
):
    copies = [
        pltpu.make_async_copy(source, target, sems.at[i])
        for i, (source, target) in enumerate(
            (
                (table_hbm.at[pl.ds(8 * NA, 6 * NA)], waves_ref),
                (table_hbm.at[pl.ds(0, 8 * NA)], table_ref),
            )
        )
    ]
    copies[0].start()
    phase = lax.broadcasted_iota(jnp.int32, (8, LO), 0) * lax.broadcasted_iota(jnp.int32, (8, LO), 1)
    angle = phase.astype(F32) * (math.pi / SEG)
    turns = (jnp.cos(angle), jnp.sin(angle))
    for p in range(PAIRS):
        for i in range(2):
            turn_ref[i, p] = jnp.broadcast_to(turns[i][p : p + 1], (8, LO))
    rows = fixed_ref.shape[1]
    share = rows - chans
    lead = 2 * chans
    segs = files * TD // SEG
    per_seg = files // segs
    devices = files * wins

    first = data_ref[0, chans : 2 * chans, :].astype(F32)
    row = lax.broadcasted_iota(jnp.int32, (TAPS, 128), 0)
    lane = lax.broadcasted_iota(jnp.int32, (TAPS, 128), 1)
    taps = jnp.where(lane[:1] < 32, pltpu.roll(first[:1], 32, 1), pltpu.roll(first[1:2], 64, 1))
    share_of = jnp.where(lane < TAPS, jnp.broadcast_to(taps, (TAPS, 128)), 0.0)
    for bit in range(6):
        move = (TAPS - row) >> bit
        share_of = jnp.where(move % 2 == 1, pltpu.roll(share_of, 128 - (1 << bit), 1), share_of)
    share_of = jnp.where((lane < row) & (row > 0), share_of, 0.0).astype(BF16)
    nothing = jnp.zeros((TAPS, 128), BF16)
    row = lax.broadcasted_iota(jnp.int32, (128, 128), 0)
    lane = lax.broadcasted_iota(jnp.int32, (128, 128), 1)
    columns = [
        jnp.concatenate([share_of, nothing], axis=0),
        jnp.concatenate([nothing, share_of], axis=0),
        jnp.where(row == 0, 1.0, 0.0).astype(BF16),
    ]
    for i in range(rows // chans):
        columns.append(
            jnp.where((row == 64 + EARLY * i + lane) & (lane < EARLY), 1.0, 0.0).astype(BF16)
        )
    collapse = jnp.where((row // R == lane) & (lane < EARLY), 1.0, 0.0).astype(BF16)
    tails = data_ref[:, :lead, :].reshape(devices * lead, 128)
    mixed = jnp.dot(tails, jnp.concatenate(columns, axis=1), preferred_element_type=F32)
    mixed = mixed.reshape(devices, lead, len(columns) * 128)
    residue = (lax.broadcasted_iota(jnp.int32, (1, 1, 128), 2) % R).astype(F32)
    offset = mixed[wins:, :, 256:384]

    def early(value, kept):
        value = jnp.where(residue == offset[:, :kept], value[:-wins, :kept], 0.0)
        value = value.reshape((devices - wins) * kept, 128)
        high, low = split(value)
        value = jnp.dot(high, collapse, preferred_element_type=F32) + jnp.dot(
            low, collapse, preferred_element_type=F32
        )
        value = value.reshape(devices - wins, kept, 128)
        return jnp.concatenate([jnp.zeros((wins, kept, 128), F32), value], axis=0)

    added = jnp.concatenate(
        [early(mixed[:, :, :128], share), early(mixed[:, :, 128:256], chans)], axis=1
    )
    lows = jnp.concatenate(
        [
            mixed[:, chans:, 128 * (3 + i) : 128 * (4 + i)]
            for i in range(rows // chans)
        ],
        axis=1,
    )
    fixed_ref[...] = (data_ref[:, lead:, :].astype(F32) + (lows + added)).astype(BF16).astype(F32)

    for win in range(wins):
        for seg in range(segs):
            base = (win * segs + seg) * rows
            for h in range(HALF):
                x = [fixed_ref[(seg * per_seg + HALF * n + h) * wins + win] for n in range(NN)]
                terms = spread(x)
                for p in range(PAIRS):
                    if p:
                        re, im = terms[p]
                        c = turn_ref[0, p, :1, 128 * h : 128 * h + 128]
                        s = turn_ref[1, p, :1, 128 * h : 128 * h + 128]
                        re, im = re * c + im * s, im * c - re * s
                    else:
                        re, im = terms[0][0], terms[PAIRS][0]
                    for part, value in enumerate((re, im)):
                        at = slice(128 * h, 128 * h + 128)
                        high, low = split(value)
                        high_ref[part, p, base : base + rows, at] = high
                        low_ref[part, p, base : base + rows, at] = low
    groups = wins * segs
    count = groups * rows
    copies[0].wait()
    copies[1].start()

    def product(part, first, last, begin, end):
        lines = (last - first) * count
        return three_pass(
            high_ref[part, first:last].reshape(lines, LO),
            low_ref[part, first:last].reshape(lines, LO),
            waves_ref[begin * NA : end * NA, :LO],
            waves_ref[begin * NA : end * NA, LO:],
            NT,
        ).reshape(last - first, count, (end - begin) * NA)

    for part, begin in enumerate((0, 4)):
        value = product(part, 0, 1, begin, begin + 2)[0]
        spec_ref[0, :, 2 * NA * part : 2 * NA * part + NA] = value[:, :NA]
        spec_ref[0, :, 2 * NA * part + NA : 2 * NA * (part + 1)] = -value[:, NA:]
    of_re = product(0, 1, PAIRS, 0, 4)
    of_im = product(1, 1, PAIRS, 0, 4)
    c, s, cc, ss = (slice(NA * i, NA * (i + 1)) for i in range(4))
    spec_ref[1:, :, c] = of_re[..., c] + of_im[..., s]
    spec_ref[1:, :, s] = of_im[..., c] - of_re[..., s]
    spec_ref[1:, :, cc] = of_re[..., cc] - of_im[..., ss]
    spec_ref[1:, :, ss] = -(of_im[..., cc] + of_re[..., ss])
    total = jnp.zeros((count, NA), F32)
    for p in range(PAIRS):
        for part in range(2):
            re = spec_ref[p, :, 2 * NA * part : 2 * NA * part + NA]
            im = spec_ref[p, :, 2 * NA * part + NA : 2 * NA * part + 2 * NA]
            total += jnp.sqrt(re * re + im * im)
    high, low = split(total)
    low2 = (total - high.astype(F32) - low.astype(F32)).astype(BF16)
    row = lax.broadcasted_iota(jnp.int32, (NA, NA), 0)
    lane = lax.broadcasted_iota(jnp.int32, (NA, NA), 1)
    per_band = BAND // PH
    band = jnp.where(row // per_band == lane // per_band, 1.0, 0.0).astype(BF16)
    amplitude = (
        jnp.dot(
            jnp.concatenate([high, low, low2], axis=1),
            jnp.concatenate([band] * 3, axis=0),
            preferred_element_type=F32,
        )
        * (1.0 / BAND)
        + EPSILON
    )
    gain = 1.0 / amplitude
    gain = jnp.concatenate([gain] * 4, axis=1)
    for group in range(groups):
        at = slice(group * rows, group * rows + share)
        own = slice(group * rows + share, (group + 1) * rows)
        for p in range(PAIRS):
            src_ref[p, group] = (spec_ref[p, at] * gain[at]).astype(BF16)
            own_ref[p, group] = (spec_ref[p, own] * gain[own]).astype(BF16).astype(F32) * scale
    copies[1].wait()


def gather_lags(ends, re, im):
    half = PH // 2
    quarter = half // 2
    both = [None] + [re[p] + re[half - p] for p in range(1, quarter)]
    apart = [None] + [re[p] - re[half - p] for p in range(1, quarter)]
    oboth = [None] + [im[p] + im[half - p] for p in range(1, quarter)]
    oapart = [None] + [im[p] - im[half - p] for p in range(1, quarter)]
    edge = (ends[0] + ends[1], ends[0] - ends[1])
    cosines, sines = {}, {}
    for n in range(NN // 2 + 1):
        fold, total = (both, edge[0]) if n % 2 == 0 else (apart, edge[1])
        if n % 2 == 0:
            total = total + re[quarter] if (n // 2) % 2 == 0 else total - re[quarter]
        for p in range(1, quarter):
            c = math.cos(2 * math.pi * p * n / PH)
            if abs(abs(c) - 1) < 1e-9:
                total = total + fold[p] if c > 0 else total - fold[p]
            elif abs(c) > 1e-9:
                total = total + fold[p] * c
        cosines[n] = total
        if n:
            ofold = oapart if n % 2 == 0 else oboth
            total = None
            for p in range(1, quarter):
                s = math.sin(2 * math.pi * p * n / PH)
                if abs(s) > 1e-9:
                    term = ofold[p] if abs(s - 1) < 1e-9 else -ofold[p] if abs(s + 1) < 1e-9 else ofold[p] * s
                    total = term if total is None else total + term
            if n % 2:
                total = total + im[quarter] if n % 4 == 1 else total - im[quarter]
            sines[n] = total
    lags = []
    for n in range(-NN // 2, NN // 2):
        if n == 0:
            lags.append(cosines[0])
        else:
            lags.append(cosines[-n] + sines[-n] if n < 0 else cosines[n] - sines[n])
    return lags


def pair_kernel(last, group_size, own_ref, src_ref, table_ref, turn_ref, *refs):
    if last:
        done_ref, out_hbm, wide_ref, pair_a, pair_b, lag_a, lag_b, out_ref, sems = refs
    else:
        out_ref, wide_ref, pair_a, pair_b, lag_a, lag_b = refs
    groups, chans = own_ref.shape[1:3]
    share = src_ref.shape[2]
    size = group_size * chans
    copies = []

    def write(source, place, count):
        if last:
            copies.append(
                pltpu.make_async_copy(source, out_hbm.at[pl.ds(place, count)], sems.at[len(copies)])
            )
            copies[-1].start()

    if last:
        core = lax.axis_index("file") % 2
        write(done_ref, core * share, share)
        place = (1 - core) * share
    wide_ref[...] = src_ref[...].astype(F32)

    def cross(first, pair_ref):
        for p in range(PAIRS):
            for part in range(2):
                left = 2 * NA * part
                own = [
                    (own_ref[p, g, :, left : left + NA], own_ref[p, g, :, left + NA : left + 2 * NA])
                    for g in range(groups)
                ]
                for s in range(0, group_size, 2):
                    res, ims = [], []
                    for one in range(2):
                        cre, cim = None, None
                        for g in range(groups):
                            at = first + s + one
                            sre = wide_ref[p, g, at : at + 1, left : left + NA]
                            sim = wide_ref[p, g, at : at + 1, left + NA : left + 2 * NA]
                            ore, oim = own[g]
                            tre = ore * sre + oim * sim
                            tim = oim * sre - ore * sim
                            cre = tre if cre is None else cre + tre
                            cim = tim if cim is None else cim + tim
                        res.append(cre)
                        ims.append(cim)
                    at = slice(s * chans, (s + 2) * chans)
                    pair_ref[p, at, left : left + NA] = jnp.concatenate(res, 0).astype(BF16)
                    pair_ref[p, at, left + NA : left + 2 * NA] = jnp.concatenate(ims, 0).astype(BF16)

    def product(pair_ref, lag_ref):
        lag_ref[0] = jnp.dot(pair_ref[0], table_ref[: 4 * NA], preferred_element_type=F32)
        lag_ref[1:] = jnp.dot(
            pair_ref[1:].reshape((PAIRS - 1) * size, 4 * NA),
            table_ref[4 * NA :],
            preferred_element_type=F32,
        ).reshape(PAIRS - 1, size, 2 * LO)

    def lags(first, lag_ref):
        for s in range(group_size):
            at = slice(s * chans, (s + 1) * chans)
            for h in range(HALF):
                lo = 128 * h
                ends = [lag_ref[0, at, LO * i + lo : LO * i + lo + 128] for i in range(2)]
                re, im = [None], [None]
                for p in range(1, PAIRS):
                    u = lag_ref[p, at, lo : lo + 128]
                    v = lag_ref[p, at, LO + lo : LO + lo + 128]
                    c = turn_ref[0, p, :, lo : lo + 128]
                    d = turn_ref[1, p, :, lo : lo + 128]
                    re.append(c * u - d * v)
                    im.append(c * v + d * u)
                for n, value in enumerate(gather_lags(ends, re, im)):
                    out_ref[first + s, :, LO * n + lo : LO * n + lo + 128] = value
            if last:
                write(out_ref.at[pl.ds(first + s, 1)], place + first + s, 1)

    steps = share // group_size
    pairs, lagged = (pair_a, pair_b), (lag_a, lag_b)
    cross(0, pair_a)
    for i in range(steps):
        product(pairs[i % 2], lagged[i % 2])
        if i + 1 < steps:
            cross((i + 1) * group_size, pairs[(i + 1) % 2])
        if i:
            lags((i - 1) * group_size, lagged[(i - 1) % 2])
    lags((steps - 1) * group_size, lagged[(steps - 1) % 2])
    for copy in copies:
        copy.wait()


def pair_call(own, src, table, turn, done=None):
    groups, chans = own.shape[1:3]
    share = src.shape[2]
    vmem = pl.BlockSpec(memory_space=pltpu.VMEM)
    hbm = pl.BlockSpec(memory_space=pltpu.HBM)
    last = done is not None
    group_size = min(GROUPS[last], share)
    operands = [own, src, table, turn] + [done] * last
    scratch = [pltpu.VMEM((PAIRS, groups, share, 4 * NA), F32)]
    scratch += [pltpu.VMEM((PAIRS, group_size * chans, 4 * NA), BF16)] * 2
    scratch += [pltpu.VMEM((PAIRS, group_size * chans, 2 * LO), F32)] * 2
    if last:
        scratch += [
            pltpu.VMEM((share, chans, SEG), F32),
            pltpu.SemaphoreType.DMA((1 + share,)),
        ]
    return pl.pallas_call(
        functools.partial(pair_kernel, last, group_size),
        in_specs=[vmem] * len(operands),
        out_specs=hbm if last else vmem,
        scratch_shapes=scratch,
        out_shape=jax.ShapeDtypeStruct((share * (2 if last else 1), chans, SEG), F32),
        compiler_params=pltpu.CompilerParams(vmem_limit_bytes=32 * 2**20),
        name="pair_last" if last else "pair_first",
    )(*operands)


def local(raw, fir_taps, offsets, vs_index):
    samples = raw[0]
    channels = samples.shape[0]
    files = lax.axis_size("file")
    wins = lax.axis_size("win")
    sources = vs_index.shape[0] // wins
    share = sources // 2
    chans = channels // files
    rows = share + chans
    segs = files * TD // SEG
    groups = wins * segs
    taps = fir_taps[None, :]
    index = vs_index[None, :]
    table = transform_table()
    scale = 1.0 / math.sqrt(SEG * segs * wins)
    hbm = pl.BlockSpec(memory_space=pltpu.HBM)
    vmem = pl.BlockSpec(memory_space=pltpu.VMEM)
    packed = pl.pallas_call(
        functools.partial(decimate_kernel, files, wins),
        out_shape=jax.ShapeDtypeStruct((files * wins, 2 * chans + rows, TD), BF16),
        in_specs=[hbm] * 4,
        out_specs=vmem,
        scratch_shapes=[
            pltpu.SMEM(offsets.shape, jnp.int32),
            pltpu.VMEM(taps.shape, F32),
            pltpu.VMEM(index.shape, jnp.int32),
            pltpu.VMEM(samples.shape, BF16),
            pltpu.SemaphoreType.DMA((4,)),
        ],
        compiler_params=pltpu.CompilerParams(vmem_limit_bytes=60 * 2**20),
        name="decimate",
    )(offsets, taps, index, samples)
    data = lax.all_to_all(packed, ("file", "win"), split_axis=0, concat_axis=0, tiled=True)
    own, src, table_high, turn = pl.pallas_call(
        functools.partial(forward_kernel, files, wins, chans, scale),
        out_shape=(
            jax.ShapeDtypeStruct((PAIRS, groups, chans, 4 * NA), F32),
            jax.ShapeDtypeStruct((PAIRS, groups, share, 4 * NA), BF16),
            jax.ShapeDtypeStruct((8 * NA, 2 * LO), BF16),
            jax.ShapeDtypeStruct((2, PAIRS, 8, LO), F32),
        ),
        in_specs=[vmem, hbm],
        out_specs=(vmem, vmem, vmem, vmem),
        scratch_shapes=[
            pltpu.VMEM((6 * NA, 2 * LO), BF16),
            pltpu.VMEM((files * wins, rows, TD), F32),
            pltpu.VMEM((2, PAIRS, groups * rows, LO), BF16),
            pltpu.VMEM((2, PAIRS, groups * rows, LO), BF16),
            pltpu.VMEM((PAIRS, groups * rows, 4 * NA), F32),
            pltpu.SemaphoreType.DMA((2,)),
        ],
        compiler_params=pltpu.CompilerParams(vmem_limit_bytes=103 * 2**19),
        name="forward",
    )(data, table)
    other = lax.ppermute(src, "file", [(i, i ^ 1) for i in range(files)])
    half = pair_call(own, src, table_high, turn)
    return pair_call(own, other, table_high, turn, half)


def solution(mesh):
    return jax.shard_map(
        local,
        mesh=mesh,
        in_specs=(P("win", None, "file"), P(), P("win", "file"), P()),
        out_specs=P("win", "file", None),
        check_vma=False,
    )
```

```python
import functools
import math

import jax
import jax.numpy as jnp
import numpy as np
from jax import lax
from jax.experimental import pallas as pl
from jax.experimental.pallas import tpu as pltpu
from jax.sharding import PartitionSpec as P

R = 10
TAPS = 64
TD = 128
SEG = 2048
BAND = 64
EPSILON = 1e-06

PH = 16
LO = 256
NA = SEG // PH
NN = SEG // LO
HALF = LO // 128
PAIRS = PH // 2
EARLY = 8
GROUPS = (8, 8)
TABLE_ROWS = 2048

NT = (((1,), (1,)), ((), ()))
NN_DIMS = (((1,), (0,)), ((), ()))
F32 = jnp.float32
BF16 = jnp.bfloat16


def transform_table():
    a = np.arange(NA)[:, None]
    m = np.arange(LO)[None, :]

    def wave(f):
        angle = 2 * np.pi * ((f * m) % (2 * SEG)) / (2 * SEG)
        return np.cos(angle), np.sin(angle)

    c, s = wave(PH * a)
    cc, ss = wave(PH * (a + 1))
    folded = np.block([[c, s], [-s, c], [cc, -ss], [-ss, -cc]])
    c8, s8 = wave(PH * a + PH // 2)
    z = np.zeros_like(c)
    ends = np.block([[c, z], [-s, z], [z, c8], [z, -s8]])
    waves = np.concatenate([c, s, cc, ss, c8, s8])
    high = waves.astype(BF16)
    low = (waves - high.astype(np.float64)).astype(BF16)
    inverse = np.concatenate([ends, folded]).astype(BF16)
    parts = [inverse, np.concatenate([high, low], axis=1)]
    spare = TABLE_ROWS - sum(len(part) for part in parts)
    return jnp.asarray(np.concatenate(parts + [np.zeros((spare, 2 * LO), BF16)]))


def three_pass(high, low, table_high, table_low, dims):
    dot = functools.partial(lax.dot_general, dimension_numbers=dims, preferred_element_type=F32)
    return dot(high, table_high) + (dot(low, table_high) + dot(high, table_low))


def split(x):
    high = x.astype(BF16)
    return high, (x - high.astype(F32)).astype(BF16)


def decimate_kernel(
    files, wins,
    offset_hbm, taps_hbm, index_hbm, raw_hbm, out_ref,
    offset_ref, taps_ref, index_ref, raw_ref, sems,
):
    copies = [
        pltpu.make_async_copy(source, target, sems.at[i])
        for i, (source, target) in enumerate(
            (
                (offset_hbm, offset_ref),
                (taps_hbm, taps_ref),
                (index_hbm, index_ref),
                (raw_hbm, raw_ref),
            )
        )
    ]
    for copy in copies:
        copy.start()
    channels, samples = raw_ref.shape
    half = TD // 2
    stride = R * half
    width = stride + 128
    copies[0].wait()
    copies[1].wait()
    offset = offset_ref[0, 0]
    taps = jnp.broadcast_to(taps_ref[...], (half, TAPS)).astype(BF16)
    k = lax.broadcasted_iota(jnp.int32, (TAPS, 256), 0)
    lane = lax.broadcasted_iota(jnp.int32, (TAPS, 256), 1)
    place = jnp.where(lane == 128 - k, 1.0, 0.0).astype(BF16)
    band = jnp.dot(taps, place, preferred_element_type=F32)
    band = pltpu.roll(band[:8], offset, 1)
    row = lax.broadcasted_iota(jnp.int32, (8, 256), 0)
    for bit in range(3):
        band = jnp.where((row >> bit) % 2 == 1, pltpu.roll(band, R << bit, 1), band)
    band = jnp.concatenate([band, jnp.zeros((8, width - 256), F32)], axis=1)
    tiles = [band if not i else pltpu.roll(band, 8 * R * i, 1) for i in range(half // 8)]
    rolled = jnp.concatenate(tiles, axis=0).astype(BF16)
    zero = jnp.zeros((half, width), BF16)
    first = jnp.concatenate([rolled, zero], axis=0)
    second = jnp.concatenate([zero, rolled], axis=0)
    copies[2].wait()
    sources = index_ref.shape[1]
    row = lax.broadcasted_iota(jnp.int32, (channels, sources), 0)
    pick = jnp.where(row == index_ref[...], 1.0, 0.0).astype(BF16)
    copies[3].wait()
    total = lax.dot_general(
        raw_ref[:, stride - 128 : 2 * stride], second, NT, preferred_element_type=F32
    )
    total += lax.dot_general(raw_ref[:, :stride], first[:, 128:], NT, preferred_element_type=F32)
    decimated = total.astype(BF16)
    lane = lax.broadcasted_iota(jnp.int32, (channels, 128), 1)
    low = jnp.where(lane < EARLY, total - decimated.astype(F32), 0.0)
    tail = raw_ref[:, samples - 128 :].astype(F32)
    tail = jnp.where(lane == TAPS, offset.astype(F32), tail)
    everything = jnp.concatenate([decimated, tail.astype(BF16), low.astype(BF16)], axis=1)
    chosen = lax.dot_general(
        pick, everything, (((0,), (0,)), ((), ())), preferred_element_type=F32
    )
    per_win = sources // wins
    share = per_win // 2
    per_file = channels // files
    lower = lane[:per_file] < 64

    def low_lanes(value, i):
        return pltpu.roll(value, 64 + EARLY * i, 1)

    wide = jnp.concatenate([taps_ref[...], jnp.zeros((1, 128 - TAPS), F32)], axis=1)
    row = lax.broadcasted_iota(jnp.int32, (per_file, 128), 0)
    carried = jnp.where(row == 0, pltpu.roll(wide, 96, 1), pltpu.roll(wide, 64, 1))
    carried = jnp.where((row < 2) & (lane[:per_file] >= 96), carried, 0.0)
    blocks = {}
    for win in range(wins):
        for core in range(2):
            at = win * per_win + core * share
            part = chosen[at : at + share]
            tails = pltpu.roll(part[:, 128:256], 64, 1)
            lows = part[:, 256:]
            packed = carried + low_lanes(lows[:per_file], 0)
            for i in range(1, share // per_file):
                packed += low_lanes(lows[i * per_file : (i + 1) * per_file], i)
            second = tails[per_file:] if share > per_file else jnp.zeros_like(packed)
            blocks[win, core] = (
                part[:, :128].astype(BF16), tails[:per_file], jnp.where(lower, second, packed)
            )
    for file in range(files):
        own = slice(file * per_file, (file + 1) * per_file)
        own_low = low_lanes(low[own], share // per_file)
        for win in range(wins):
            dest = file * wins + win
            dec, tails, packed = blocks[win, file % 2]
            out_ref[dest, : 2 * per_file, :] = jnp.concatenate(
                [jnp.where(lower, tails, tail[own]), packed + own_low], axis=0
            ).astype(BF16)
            out_ref[dest, 2 * per_file : 2 * per_file + share, :] = dec
            out_ref[dest, 2 * per_file + share :, :] = decimated[own]


def spread(x):
    terms = []
    for p in range(PH // 2 + 1):
        re, im = None, None
        for n in range(NN):
            angle = (p * n) % PH
            c, s = math.cos(2 * math.pi * angle / PH), -math.sin(2 * math.pi * angle / PH)
            if angle % (PH // 4):
                re = x[n] * c if re is None else re + x[n] * c
                im = x[n] * s if im is None else im + x[n] * s
            elif angle % (PH // 2):
                im = x[n] * round(s) if im is None else (im + x[n] if s > 0 else im - x[n])
            else:
                re = x[n] if re is None else (re + x[n] if c > 0 else re - x[n])
        terms.append((re, im))
    return terms


def forward_kernel(
    files, wins, chans, scale,
    data_ref, table_hbm, own_ref, src_ref, table_ref, turn_ref,
    waves_ref, fixed_ref, split_ref, spec_ref, sems,
):
    copies = [
        pltpu.make_async_copy(source, target, sems.at[i])
        for i, (source, target) in enumerate(
            (
                (table_hbm.at[pl.ds(8 * NA, 6 * NA)], waves_ref),
                (table_hbm.at[pl.ds(0, 8 * NA)], table_ref),
            )
        )
    ]
    copies[0].start()
    phase = lax.broadcasted_iota(jnp.int32, (8, LO), 0) * lax.broadcasted_iota(jnp.int32, (8, LO), 1)
    angle = phase.astype(F32) * (math.pi / SEG)
    turns = (jnp.cos(angle), jnp.sin(angle))
    for p in range(PAIRS):
        for i in range(2):
            turn_ref[i, p] = jnp.broadcast_to(turns[i][p : p + 1], (8, LO))
    rows = fixed_ref.shape[1]
    share = rows - chans
    lead = 2 * chans
    segs = files * TD // SEG
    per_seg = files // segs
    devices = files * wins

    first = data_ref[0, chans : 2 * chans, :].astype(F32)
    row = lax.broadcasted_iota(jnp.int32, (TAPS, 128), 0)
    lane = lax.broadcasted_iota(jnp.int32, (TAPS, 128), 1)
    taps = jnp.where(lane[:1] < 32, pltpu.roll(first[:1], 32, 1), pltpu.roll(first[1:2], 64, 1))
    share_of = jnp.where(lane < TAPS, jnp.broadcast_to(taps, (TAPS, 128)), 0.0)
    for bit in range(6):
        move = (TAPS - row) >> bit
        share_of = jnp.where(move % 2 == 1, pltpu.roll(share_of, 128 - (1 << bit), 1), share_of)
    share_of = jnp.where((lane < row) & (row > 0), share_of, 0.0).astype(BF16)
    nothing = jnp.zeros((TAPS, 128), BF16)
    row = lax.broadcasted_iota(jnp.int32, (128, 128), 0)
    lane = lax.broadcasted_iota(jnp.int32, (128, 128), 1)
    columns = [
        jnp.concatenate([share_of, nothing], axis=0),
        jnp.concatenate([nothing, share_of], axis=0),
        jnp.where(row == 0, 1.0, 0.0).astype(BF16),
    ]
    for i in range(rows // chans):
        columns.append(
            jnp.where((row == 64 + EARLY * i + lane) & (lane < EARLY), 1.0, 0.0).astype(BF16)
        )
    collapse = jnp.where((row // R == lane) & (lane < EARLY), 1.0, 0.0).astype(BF16)
    tails = data_ref[:, :lead, :].reshape(devices * lead, 128)
    mixed = jnp.dot(tails, jnp.concatenate(columns, axis=1), preferred_element_type=F32)
    mixed = mixed.reshape(devices, lead, len(columns) * 128)
    residue = (lax.broadcasted_iota(jnp.int32, (1, 1, 128), 2) % R).astype(F32)
    offset = mixed[wins:, :, 256:384]

    def early(value, kept):
        value = jnp.where(residue == offset[:, :kept], value[:-wins, :kept], 0.0)
        value = value.reshape((devices - wins) * kept, 128)
        high, low = split(value)
        value = jnp.dot(high, collapse, preferred_element_type=F32) + jnp.dot(
            low, collapse, preferred_element_type=F32
        )
        value = value.reshape(devices - wins, kept, 128)
        return jnp.concatenate([jnp.zeros((wins, kept, 128), F32), value], axis=0)

    added = jnp.concatenate(
        [early(mixed[:, :, :128], share), early(mixed[:, :, 128:256], chans)], axis=1
    )
    lows = jnp.concatenate(
        [
            mixed[:, chans:, 128 * (3 + i) : 128 * (4 + i)]
            for i in range(rows // chans)
        ],
        axis=1,
    )
    fixed_ref[...] = (data_ref[:, lead:, :].astype(F32) + (lows + added)).astype(BF16).astype(F32)

    for win in range(wins):
        for seg in range(segs):
            base = (win * segs + seg) * rows
            for h in range(HALF):
                x = [fixed_ref[(seg * per_seg + HALF * n + h) * wins + win] for n in range(NN)]
                terms = spread(x)
                for p in range(PAIRS):
                    if p:
                        re, im = terms[p]
                        c = turn_ref[0, p, :1, 128 * h : 128 * h + 128]
                        s = turn_ref[1, p, :1, 128 * h : 128 * h + 128]
                        re, im = re * c + im * s, im * c - re * s
                    else:
                        re, im = terms[0][0], terms[PAIRS][0]
                    for part, value in enumerate((re, im)):
                        at = slice(128 * h, 128 * h + 128)
                        high, low = split(value)
                        split_ref[0, part, p, base : base + rows, at] = high
                        split_ref[1, part, p, base : base + rows, at] = low
    groups = wins * segs
    count = groups * rows
    copies[0].wait()
    copies[1].start()

    def product(part, first, last, begin, end):
        lines = (last - first) * count
        return three_pass(
            split_ref[0, part, first:last].reshape(lines, LO),
            split_ref[1, part, first:last].reshape(lines, LO),
            waves_ref[begin * NA : end * NA, :LO],
            waves_ref[begin * NA : end * NA, LO:],
            NT,
        ).reshape(last - first, count, (end - begin) * NA)

    for part, begin in enumerate((0, 4)):
        value = product(part, 0, 1, begin, begin + 2)[0]
        spec_ref[0, :, 2 * NA * part : 2 * NA * part + NA] = value[:, :NA]
        spec_ref[0, :, 2 * NA * part + NA : 2 * NA * (part + 1)] = -value[:, NA:]
    dot = functools.partial(lax.dot_general, dimension_numbers=NT, preferred_element_type=F32)
    lines = 2 * (PAIRS - 1) * count
    table = waves_ref[: 4 * NA, :LO]
    both = dot(split_ref[:, :, 1:].reshape(2 * lines, LO), table)
    rest = dot(split_ref[0, :, 1:].reshape(lines, LO), waves_ref[: 4 * NA, LO:])
    of_both = (both[:lines] + (both[lines:] + rest)).reshape(2, PAIRS - 1, count, 4 * NA)
    of_re, of_im = of_both[0], of_both[1]
    c, s, cc, ss = (slice(NA * i, NA * (i + 1)) for i in range(4))
    spec_ref[1:, :, c] = of_re[..., c] + of_im[..., s]
    spec_ref[1:, :, s] = of_im[..., c] - of_re[..., s]
    spec_ref[1:, :, cc] = of_re[..., cc] - of_im[..., ss]
    spec_ref[1:, :, ss] = -(of_im[..., cc] + of_re[..., ss])
    total = jnp.zeros((count, NA), F32)
    for p in range(PAIRS):
        for part in range(2):
            re = spec_ref[p, :, 2 * NA * part : 2 * NA * part + NA]
            im = spec_ref[p, :, 2 * NA * part + NA : 2 * NA * part + 2 * NA]
            total += jnp.sqrt(re * re + im * im)
    high, low = split(total)
    low2 = (total - high.astype(F32) - low.astype(F32)).astype(BF16)
    row = lax.broadcasted_iota(jnp.int32, (NA, NA), 0)
    lane = lax.broadcasted_iota(jnp.int32, (NA, NA), 1)
    per_band = BAND // PH
    band = jnp.where(row // per_band == lane // per_band, 1.0, 0.0).astype(BF16)
    amplitude = (
        jnp.dot(
            jnp.concatenate([high, low, low2], axis=1),
            jnp.concatenate([band] * 3, axis=0),
            preferred_element_type=F32,
        )
        * (1.0 / BAND)
        + EPSILON
    )
    gain = 1.0 / amplitude
    gain = jnp.concatenate([gain] * 4, axis=1)
    for group in range(groups):
        at = slice(group * rows, group * rows + share)
        own = slice(group * rows + share, (group + 1) * rows)
        for p in range(PAIRS):
            src_ref[p, group] = (spec_ref[p, at] * gain[at]).astype(BF16)
            own_ref[p, group] = (spec_ref[p, own] * gain[own]).astype(BF16).astype(F32) * scale
    copies[1].wait()


def gather_lags(ends, re, im):
    half = PH // 2
    quarter = half // 2
    both = [None] + [re[p] + re[half - p] for p in range(1, quarter)]
    apart = [None] + [re[p] - re[half - p] for p in range(1, quarter)]
    oboth = [None] + [im[p] + im[half - p] for p in range(1, quarter)]
    oapart = [None] + [im[p] - im[half - p] for p in range(1, quarter)]
    edge = (ends[0] + ends[1], ends[0] - ends[1])
    cosines, sines = {}, {}
    for n in range(NN // 2 + 1):
        fold, total = (both, edge[0]) if n % 2 == 0 else (apart, edge[1])
        if n % 2 == 0:
            total = total + re[quarter] if (n // 2) % 2 == 0 else total - re[quarter]
        for p in range(1, quarter):
            c = math.cos(2 * math.pi * p * n / PH)
            if abs(abs(c) - 1) < 1e-9:
                total = total + fold[p] if c > 0 else total - fold[p]
            elif abs(c) > 1e-9:
                total = total + fold[p] * c
        cosines[n] = total
        if n:
            ofold = oapart if n % 2 == 0 else oboth
            total = None
            for p in range(1, quarter):
                s = math.sin(2 * math.pi * p * n / PH)
                if abs(s) > 1e-9:
                    term = ofold[p] if abs(s - 1) < 1e-9 else -ofold[p] if abs(s + 1) < 1e-9 else ofold[p] * s
                    total = term if total is None else total + term
            if n % 2:
                total = total + im[quarter] if n % 4 == 1 else total - im[quarter]
            sines[n] = total
    lags = []
    for n in range(-NN // 2, NN // 2):
        if n == 0:
            lags.append(cosines[0])
        else:
            lags.append(cosines[-n] + sines[-n] if n < 0 else cosines[n] - sines[n])
    return lags


def pair_kernel(last, group_size, own_ref, src_ref, table_ref, turn_ref, *refs):
    if last:
        done_ref, out_hbm, wide_ref, pair_a, pair_b, lag_a, lag_b, out_ref, sems = refs
    else:
        out_ref, wide_ref, pair_a, pair_b, lag_a, lag_b = refs
    groups, chans = own_ref.shape[1:3]
    share = src_ref.shape[2]
    size = group_size * chans
    copies = []

    def write(source, place, count):
        if last:
            copies.append(
                pltpu.make_async_copy(source, out_hbm.at[pl.ds(place, count)], sems.at[len(copies)])
            )
            copies[-1].start()

    if last:
        core = lax.axis_index("file") % 2
        write(done_ref, core * share, share)
        place = (1 - core) * share
    wide_ref[...] = src_ref[...].astype(F32)

    def cross(first, pair_ref):
        for p in range(PAIRS):
            for part in range(2):
                left = 2 * NA * part
                own = [
                    (own_ref[p, g, :, left : left + NA], own_ref[p, g, :, left + NA : left + 2 * NA])
                    for g in range(groups)
                ]
                for s in range(0, group_size, 2):
                    res, ims = [], []
                    for one in range(2):
                        cre, cim = None, None
                        for g in range(groups):
                            at = first + s + one
                            sre = wide_ref[p, g, at : at + 1, left : left + NA]
                            sim = wide_ref[p, g, at : at + 1, left + NA : left + 2 * NA]
                            ore, oim = own[g]
                            tre = ore * sre + oim * sim
                            tim = oim * sre - ore * sim
                            cre = tre if cre is None else cre + tre
                            cim = tim if cim is None else cim + tim
                        res.append(cre)
                        ims.append(cim)
                    at = slice(s * chans, (s + 2) * chans)
                    pair_ref[p, at, left : left + NA] = jnp.concatenate(res, 0).astype(BF16)
                    pair_ref[p, at, left + NA : left + 2 * NA] = jnp.concatenate(ims, 0).astype(BF16)

    def product(pair_ref, lag_ref):
        lag_ref[0] = jnp.dot(pair_ref[0], table_ref[: 4 * NA], preferred_element_type=F32)
        lag_ref[1:] = jnp.dot(
            pair_ref[1:].reshape((PAIRS - 1) * size, 4 * NA),
            table_ref[4 * NA :],
            preferred_element_type=F32,
        ).reshape(PAIRS - 1, size, 2 * LO)

    def lags(first, lag_ref):
        for s in range(group_size):
            at = slice(s * chans, (s + 1) * chans)
            for h in range(HALF):
                lo = 128 * h
                ends = [lag_ref[0, at, LO * i + lo : LO * i + lo + 128] for i in range(2)]
                re, im = [None], [None]
                for p in range(1, PAIRS):
                    u = lag_ref[p, at, lo : lo + 128]
                    v = lag_ref[p, at, LO + lo : LO + lo + 128]
                    c = turn_ref[0, p, :, lo : lo + 128]
                    d = turn_ref[1, p, :, lo : lo + 128]
                    re.append(c * u - d * v)
                    im.append(c * v + d * u)
                for n, value in enumerate(gather_lags(ends, re, im)):
                    out_ref[first + s, :, LO * n + lo : LO * n + lo + 128] = value
            if last:
                write(out_ref.at[pl.ds(first + s, 1)], place + first + s, 1)

    steps = share // group_size
    pairs, lagged = (pair_a, pair_b), (lag_a, lag_b)
    cross(0, pair_a)
    for i in range(steps):
        product(pairs[i % 2], lagged[i % 2])
        if i + 1 < steps:
            cross((i + 1) * group_size, pairs[(i + 1) % 2])
        if i:
            lags((i - 1) * group_size, lagged[(i - 1) % 2])
    lags((steps - 1) * group_size, lagged[(steps - 1) % 2])
    for copy in copies:
        copy.wait()


def pair_call(own, src, table, turn, done=None):
    groups, chans = own.shape[1:3]
    share = src.shape[2]
    vmem = pl.BlockSpec(memory_space=pltpu.VMEM)
    hbm = pl.BlockSpec(memory_space=pltpu.HBM)
    last = done is not None
    group_size = min(GROUPS[last], share)
    operands = [own, src, table, turn] + [done] * last
    scratch = [pltpu.VMEM((PAIRS, groups, share, 4 * NA), F32)]
    scratch += [pltpu.VMEM((PAIRS, group_size * chans, 4 * NA), BF16)] * 2
    scratch += [pltpu.VMEM((PAIRS, group_size * chans, 2 * LO), F32)] * 2
    if last:
        scratch += [
            pltpu.VMEM((share, chans, SEG), F32),
            pltpu.SemaphoreType.DMA((1 + share,)),
        ]
    return pl.pallas_call(
        functools.partial(pair_kernel, last, group_size),
        in_specs=[vmem] * len(operands),
        out_specs=hbm if last else vmem,
        scratch_shapes=scratch,
        out_shape=jax.ShapeDtypeStruct((share * (2 if last else 1), chans, SEG), F32),
        compiler_params=pltpu.CompilerParams(vmem_limit_bytes=32 * 2**20),
        name="pair_last" if last else "pair_first",
    )(*operands)


def local(raw, fir_taps, offsets, vs_index):
    samples = raw[0]
    channels = samples.shape[0]
    files = lax.axis_size("file")
    wins = lax.axis_size("win")
    sources = vs_index.shape[0] // wins
    share = sources // 2
    chans = channels // files
    rows = share + chans
    segs = files * TD // SEG
    groups = wins * segs
    taps = fir_taps[None, :]
    index = vs_index[None, :]
    table = transform_table()
    scale = 1.0 / math.sqrt(SEG * segs * wins)
    hbm = pl.BlockSpec(memory_space=pltpu.HBM)
    vmem = pl.BlockSpec(memory_space=pltpu.VMEM)
    packed = pl.pallas_call(
        functools.partial(decimate_kernel, files, wins),
        out_shape=jax.ShapeDtypeStruct((files * wins, 2 * chans + rows, TD), BF16),
        in_specs=[hbm] * 4,
        out_specs=vmem,
        scratch_shapes=[
            pltpu.SMEM(offsets.shape, jnp.int32),
            pltpu.VMEM(taps.shape, F32),
            pltpu.VMEM(index.shape, jnp.int32),
            pltpu.VMEM(samples.shape, BF16),
            pltpu.SemaphoreType.DMA((4,)),
        ],
        compiler_params=pltpu.CompilerParams(vmem_limit_bytes=60 * 2**20),
        name="decimate",
    )(offsets, taps, index, samples)
    data = lax.all_to_all(packed, ("file", "win"), split_axis=0, concat_axis=0, tiled=True)
    own, src, table_high, turn = pl.pallas_call(
        functools.partial(forward_kernel, files, wins, chans, scale),
        out_shape=(
            jax.ShapeDtypeStruct((PAIRS, groups, chans, 4 * NA), F32),
            jax.ShapeDtypeStruct((PAIRS, groups, share, 4 * NA), BF16),
            jax.ShapeDtypeStruct((8 * NA, 2 * LO), BF16),
            jax.ShapeDtypeStruct((2, PAIRS, 8, LO), F32),
        ),
        in_specs=[vmem, hbm],
        out_specs=(vmem, vmem, vmem, vmem),
        scratch_shapes=[
            pltpu.VMEM((6 * NA, 2 * LO), BF16),
            pltpu.VMEM((files * wins, rows, TD), F32),
            pltpu.VMEM((2, 2, PAIRS, groups * rows, LO), BF16),
            pltpu.VMEM((PAIRS, groups * rows, 4 * NA), F32),
            pltpu.SemaphoreType.DMA((2,)),
        ],
        compiler_params=pltpu.CompilerParams(vmem_limit_bytes=103 * 2**19),
        name="forward",
    )(data, table)
    other = lax.ppermute(src, "file", [(i, i ^ 1) for i in range(files)])
    half = pair_call(own, src, table_high, turn)
    return pair_call(own, other, table_high, turn, half)


def solution(mesh):
    return jax.shard_map(
        local,
        mesh=mesh,
        in_specs=(P("win", None, "file"), P(), P("win", "file"), P()),
        out_specs=P("win", "file", None),
        check_vma=False,
    )
```
